128 devices in a mesh: row: 16 (over x_hi, z, core), col: 8 (over y, x_lo).
Axes of the slice: x: 4 (x_hi: 2, x_lo: 2; x = x_hi * 2 + x_lo), y: 4, z: 4, core: 2. Of those that a mesh axis runs over, the one named last changes fastest.
Arguments:
- vector: float32 [2048, 16384], P('row', 'col')
- previous: float32 [2048, 16384], P('row', 'col'), may hold values from -6 to 6
- beta_prev: float32 [1], replicated, may hold values from 0.5 to 1.5
- hubbard_u: float32 [1], replicated, may hold values from 1 to 4
- up_patterns: float32 [16, 128, 128], replicated
- down_patterns: float32 [16, 128, 128], replicated
- up_cols: int32 [16, 12], replicated, may hold values from 0 to 15
- up_pats: int32 [16, 12], replicated, may hold values from 0 to 15
- down_cols: int32 [128, 12], replicated, may hold values from 0 to 127
- down_pats: int32 [128, 12], replicated, may hold values from 0 to 15
- up_occupied: int32 [20, 2048], P(None, 'row'), may hold values 0 or 1
- down_occupied: int32 [20, 16384], P(None, 'col'), may hold values 0 or 1
Outputs:
- next_vector: float32 [2048, 16384], P('row', 'col')
- coefficients: float32 [2], replicated
The draws below stay inside these ranges and needn't reach their ends.
All inputs are finite; a program needn't handle non-finite values. No bound on the sum of `up_occupied` or of `down_occupied` on one device may be relied on, other than what follows from the above.
Results may differ from the reference program's by a relative error of at most 0.0004.
Values sent between devices are 32-bit elements; how exact they have to be, the bound alone decides.
A program may use at most 320 MiB of HBM per device.

```python
import math
import jax
import jax.numpy as jnp
import numpy as np
from jax import lax

BLK = 128
SITES = 20
HOPS = 12
NPAT = 16
NBU = 16
NBD = 128
NU = 2048
ND = 16384


def with_diagonal(noise, diag_key, low, high):
    diag = jax.random.uniform(diag_key, (NPAT, BLK), jnp.float32, low, high)
    eye = jnp.eye(BLK, dtype=jnp.float32)
    return noise * (0.5 / math.sqrt(BLK)) + diag[:, :, None] * eye[None, :, :]


def combine_parts(rough, up_part, down_part):
    whole = rough + jnp.tile(up_part, (NU // BLK, 1)) + jnp.tile(down_part, (1, ND // BLK))
    return jnp.clip(whole, -8.0, 8.0)


def draw_vector(key, part):
    key = jax.random.fold_in(key, 7)
    rough_key, up_key, down_key = jax.random.split(key, 3)
    rough = jnp.clip(jax.random.normal(rough_key, (NU, ND), jnp.float32), -4.0, 4.0)
    up_part = jnp.clip(jax.random.normal(up_key, (BLK, ND), jnp.float32), -4.0, 4.0)
    down_part = jnp.clip(jax.random.normal(down_key, (NU, BLK), jnp.float32), -4.0, 4.0)
    return combine_parts(rough, up_part, down_part)


def draw_up_patterns(key, part):
    key = jax.random.fold_in(key, 21)
    noise_key, diag_key = jax.random.split(key)
    noise = jnp.clip(jax.random.normal(noise_key, (NPAT, BLK, BLK), jnp.float32), -4.0, 4.0)
    return with_diagonal(noise, diag_key, 0.5, 1.5)


def draw_down_patterns(key, part):
    key = jax.random.fold_in(key, 33)
    noise_key, diag_key = jax.random.split(key)
    noise = jnp.clip(jax.random.normal(noise_key, (NPAT, BLK, BLK), jnp.float32), -4.0, 4.0)
    return with_diagonal(noise, diag_key, 0.5, 1.5)


def place_ends(entries, rng, least, top_value):
    longest = entries.shape.index(max(entries.shape))
    spots = []
    for shift in (0, 1):
        where = [jax.random.randint(jax.random.fold_in(rng, axis), (), 0, length) for axis, length in enumerate(entries.shape)]
        where[longest] = (where[longest] + shift) % entries.shape[longest]
        spots.append(tuple(where))
    return entries.at[spots[0]].set(least).at[spots[1]].set(top_value)


def steps_of(stream_key, dims, shards, least, high):
    loudness, own = 1.0, jax.random.fold_in(stream_key, 6)
    for dim, shards_of in shards:
        draws = jnp.exp(jax.random.uniform(jax.random.fold_in(own, dim), (shards_of,), jnp.float32, least / len(shards), high / len(shards)))
        loudness = loudness * jnp.repeat(draws, dims[dim] // shards_of).reshape([-1 if axis == dim else 1 for axis in range(len(dims))])
    return loudness


def rank_table(count, slope):
    loads = [(1 << 20) // math.isqrt(grade ** slope) + 1 for grade in range(1, count + 1)]
    scale = 1 + sum(loads) // (1 << 30)
    return np.cumsum(np.array([max(1, weight // scale) for weight in loads]))


def ranked_ids(own_key, dims, amount, slope):
    table = rank_table(amount, slope)
    lot = jax.random.randint(jax.random.fold_in(own_key, 1), dims, 0, int(table[amount - 1]))
    standing = jnp.searchsorted(jnp.asarray(table, jnp.int32), lot, side="right")
    return jax.random.permutation(jax.random.fold_in(own_key, 2), amount)[standing].astype(jnp.int32)


def normal_values(rng, dims, spread, limit, shards=(), kind=jnp.bfloat16):
    array = jax.random.normal(rng, dims, jnp.float32) * spread
    if len(shards) > 0:
        array = steps_of(rng, dims, shards, -0.22, 0.18) * array
    return jnp.clip(array, min=-limit, max=limit).astype(kind)


def setup_inputs(seed: int = 0) -> dict:
    seeds = jax.random.split(jax.random.key(seed), 13)
    return {
        "vector": draw_vector(jax.random.fold_in(seeds[12], 71), 0),
        "previous": normal_values(seeds[1], (NU, ND), 1.0, 6.0, ((0, 16), (1, 8)), jnp.float32),
        "beta_prev": jnp.clip(jax.random.uniform(seeds[2], (1,), jnp.float32, 0.5, 1.5), 0.5, 1.5),
        "hubbard_u": jnp.clip(jnp.exp(jax.random.uniform(seeds[3], (1,), jnp.float32, math.log(1.0), math.log(4.0))), 1.0, 4.0),
        "up_patterns": draw_up_patterns(jax.random.fold_in(seeds[12], 71), 0),
        "down_patterns": draw_down_patterns(jax.random.fold_in(seeds[12], 71), 0),
        "up_cols": place_ends(jax.random.randint(seeds[6], (NBU, HOPS), 0, NBU), jax.random.fold_in(seeds[6], 1), 0, NBU - 1).astype(jnp.int32),
        "up_pats": place_ends(jax.random.randint(seeds[7], (NBU, HOPS), 0, NPAT), jax.random.fold_in(seeds[7], 1), 0, NPAT - 1).astype(jnp.int32),
        "down_cols": place_ends(ranked_ids(seeds[8], (NBD, HOPS), NBD, 1), jax.random.fold_in(seeds[8], 3), 0, NBD - 1).astype(jnp.int32),
        "down_pats": place_ends(jax.random.randint(seeds[9], (NBD, HOPS), 0, NPAT), jax.random.fold_in(seeds[9], 1), 0, NPAT - 1).astype(jnp.int32),
        "up_occupied": place_ends((jax.random.randint(seeds[10], (SITES, NU), 0, 2) < 1).astype(jnp.int32), jax.random.fold_in(seeds[10], 1), 0, 1),
        "down_occupied": place_ends((jax.random.randint(seeds[11], (SITES, ND), 0, 2) < 1).astype(jnp.int32), jax.random.fold_in(seeds[11], 1), 0, 1),
    }


def reference(vector, previous, beta_prev, hubbard_u, up_patterns, down_patterns, up_cols, up_pats, down_cols, down_pats, up_occupied, down_occupied):
    hi = lax.Precision.HIGHEST
    upper = vector.reshape(NBU, BLK, ND)
    up_term = jnp.zeros((NBU, BLK, ND), jnp.float32)
    for h in range(HOPS):
        up_term = up_term + jnp.einsum('ipq,iqd->ipd', up_patterns[up_pats[:, h]], upper[up_cols[:, h]], precision=hi)
    lower = vector.reshape(NU, NBD, BLK)
    down_term = jnp.zeros((NU, NBD, BLK), jnp.float32)
    for h in range(HOPS):
        down_term = down_term + jnp.einsum('ujq,jpq->ujp', lower[:, down_cols[:, h]], down_patterns[down_pats[:, h]], precision=hi)
    doubles = jnp.dot(up_occupied.astype(jnp.float32).T, down_occupied.astype(jnp.float32), precision=hi)
    image = up_term.reshape(NU, ND) + down_term.reshape(NU, ND) + hubbard_u[0] * doubles * vector
    alpha = jnp.sum(vector * image) / jnp.sum(vector * vector)
    residual = image - alpha * vector - beta_prev[0] * previous
    scale = jnp.sqrt(jnp.sum(residual * residual) / (NU * ND) + 1e-06)
    return (residual / scale, jnp.stack([alpha, scale]))
```

```python
import jax
import jax.numpy as jnp
from jax import lax
from jax.experimental import pallas as pl
from jax.experimental.pallas import tpu as pltpu
from jax.sharding import PartitionSpec as P

MESH = pl.DeviceIdType.MESH
f32, bf16 = jnp.float32, jnp.bfloat16
BLK = 128
HOPS = 12
NPAT = 16
ZC = [(1, 0), (3, 1), (2, 0), (1, 1), (3, 0), (2, 1), (0, 1), (0, 0)]
YX = [(1, 1), (3, 1), (2, 1), (1, 0), (0, 1), (3, 0), (2, 0), (0, 0)]


def split(x):
    hi = x.astype(bf16)
    lo = (x - hi.astype(f32)).astype(bf16)
    return hi, lo


def total_of(x):
    return jnp.sum(x, axis=(0, 1), keepdims=True)


def kernel(
    v_hbm, prev_hbm, upat_hbm, dpat_hbm, upo_hbm, dno_hbm,
    beta_ref, hub_ref, ucols, upats, dcols, dpats,
    w_hbm, coef,
    v, prev, wbuf, upat, dpat, upo, dno,
    vl, vh, x1f, x1h, x1l, x2o, x2p, dw, phl, yd,
    uo, do, ul, dl, g1, g2, g3,
    lsem, xl_s, xl_r, xh_s, xh_r, z1_s, z1_r, y1_s, y1_r, z2_s, z2_r, y2_s, y2_r,
    u_s, u_r, d_s, d_r, g1_s, g1_r, g2_s, g2_r, g3_s, g3_r,
):
    r, c = lax.axis_index("row"), lax.axis_index("col")
    xhi, s = lax.div(r, 8), lax.rem(r, 8)
    z, core = lax.div(s, 2), lax.rem(s, 2)
    y, xlo = lax.div(c, 2), lax.rem(c, 2)
    rhi = (1 - xhi) * 8 + s
    clo = y * 2 + 1 - xlo
    dev_lo, dev_x3, dev_hi = (r, clo), (rhi, clo), (rhi, c)

    def zc_to(k):
        dz, dc = ZC[k]
        return lax.rem(z + dz, 4) * 2 + lax.rem(core + dc, 2)

    def zc_from(k):
        dz, dc = ZC[k]
        return lax.rem(z + 4 - dz, 4) * 2 + lax.rem(core + 2 - dc, 2)

    def yx_to(dy, dx):
        return lax.rem(y + dy, 4) * 2 + lax.rem(xlo + dx, 2)

    def yx_from(dy, dx):
        return lax.rem(y + 4 - dy, 4) * 2 + lax.rem(xlo + 2 - dx, 2)

    def cols_of(k):
        return pl.ds(pl.multiple_of(k * 256, 256), 256)

    def rows_of(k):
        return pl.ds(pl.multiple_of(k * 16, 16), 16)

    def remote(src, dst, ssem, rsem, dev):
        return pltpu.make_async_remote_copy(
            src_ref=src, dst_ref=dst, send_sem=ssem, recv_sem=rsem, device_id=dev, device_id_type=MESH
        )

    locals_ = [
        pltpu.make_async_copy(a, b, lsem.at[i])
        for i, (a, b) in enumerate(
            [
                (v_hbm, v),
                (upat_hbm, upat),
                (dpat_hbm, dpat),
                (upo_hbm, upo),
                (dno_hbm, dno),
                (prev_hbm, prev),
            ]
        )
    ]
    barrier = pltpu.get_barrier_semaphore()
    peers = [(xhi * 8 + zc_to(k), c) for k in range(7)]
    peers += [(r, yx_to(dy, dx)) for dy, dx in YX[:7]]
    peers += [dev_x3, dev_hi]
    for dev in peers:
        pl.semaphore_signal(barrier, inc=1, device_id=dev, device_id_type=MESH)
    for cp in locals_:
        cp.start()
    pl.semaphore_wait(barrier, len(peers))

    started = []

    def go(cp):
        cp.start()
        started.append(cp)
        return cp

    to = [zc_to(k) for k in range(8)]
    frm = [zc_from(k) for k in range(8)]

    def send_x(k):
        return go(remote(v_hbm.at[:, cols_of(to[k])], vl.at[to[k]], xl_s.at[k], xl_r.at[k], dev_lo))

    xl = [send_x(0), send_x(1)]
    z1, y1 = [], []
    for k in range(7):
        z1.append(
            go(remote(v_hbm.at[:, cols_of(to[k])], x1f.at[r], z1_s.at[k], z1_r.at[k], (xhi * 8 + to[k], c)))
        )
        if k < 3:
            dy = (1, 3, 2)[k]
            cp = yx_to(dy, 0)
            y1.append(go(remote(v_hbm.at[rows_of(cp)], x2o.at[y], y1_s.at[k], y1_r.at[k], (r, cp))))

    locals_[1].wait()
    locals_[2].wait()

    def prep(t, _):
        hi, lo = split(upat[t])
        phl[t, 0:BLK] = hi
        phl[t, BLK : 2 * BLK] = lo
        hi, lo = split(dpat[t].T)
        dw[t, 0:BLK] = hi
        dw[t, BLK : 2 * BLK] = hi
        dw[t, 2 * BLK : 3 * BLK] = lo
        return 0

    lax.fori_loop(0, NPAT, prep, 0)
    locals_[0].wait()

    def make_base():
        locals_[3].wait()
        locals_[4].wait()
        ups = upo[...].astype(f32).T
        hub = hub_ref[0]

        def step(i, acc):
            cs = pl.ds(pl.multiple_of(i * 256, 256), 256)
            both = jnp.dot(ups, dno[:, cs].astype(f32), preferred_element_type=f32)
            vv = v[:, cs]
            wbuf[:, cs] = hub * both * vv
            sq = vv * vv
            return acc + sum(sq[8 * a : 8 * a + 8] for a in range(16))

        acc = lax.fori_loop(0, 8, step, jnp.zeros((8, 256), f32))
        return total_of(acc)

    def products(xs, k0s, n):
        hi, lo = split(xs)
        lhs = jnp.concatenate([hi, lo, hi], axis=1)

        def step(i, _):
            rhs = jnp.concatenate([dw[i * 4 + a] for a in range(4)], axis=1)
            out = jnp.dot(lhs, rhs, preferred_element_type=f32)
            for a in range(4):
                for b, k0 in enumerate(k0s):
                    part = out[b * n * 16 : (b + 1) * n * 16, a * BLK : (a + 1) * BLK]
                    yd[i * 4 + a, pl.ds(k0, n)] = part.reshape(n, 16, BLK)
            return 0

        lax.fori_loop(0, NPAT // 4, step, 0)

    def own_products(ysrc, ref):
        xs = jnp.concatenate([ref[:, j * BLK : (j + 1) * BLK] for j in range(16)], axis=0)
        products(xs, [(ysrc * 2 + xlo) * 16], 16)

    def lo_products(k):
        for i in range(3):
            y2[k][i].wait_recv()
        xs, k0s = [], []
        for dy in range(4):
            ysrc = lax.rem(y + 4 - dy, 4)
            if dy == 0:
                piece = vl[to[k], rows_of(c)]
            else:
                piece = x2p[ysrc, to[k]]
            xs += [piece[:, 0:BLK], piece[:, BLK : 2 * BLK]]
            k0s.append((ysrc * 2 + 1 - xlo) * 16 + to[k] * 2)
        products(jnp.concatenate(xs, axis=0), k0s, 2)

    def convert(b, x):
        hi, lo = split(x)
        x1h[b] = hi
        x1l[b] = lo

    xh, z2, y2 = [], [], []

    def relay_hi(k):
        xh[k].wait_recv()
        if k < 7:
            z2.append(go(remote(vh.at[to[k]], x1f.at[rhi], z2_s.at[k], z2_r.at[k], (xhi * 8 + to[k], c))))

    sum_vv = None
    for k in range(8):
        xl[k].wait_recv()
        if k + 2 < 8:
            xl.append(send_x(k + 2))
        xh.append(go(remote(vl.at[to[k]], vh.at[to[k]], xh_s.at[k], xh_r.at[k], dev_x3)))
        row = []
        for i, dy in enumerate((1, 3, 2)):
            cp = yx_to(dy, 0)
            row.append(
                go(remote(vl.at[to[k], rows_of(cp)], x2p.at[y, to[k]], y2_s.at[k, i], y2_r.at[k, i], (r, cp)))
            )
        y2.append(row)
        if k >= 1:
            relay_hi(k - 1)
        if k == 0:
            sum_vv = make_base()
        if k == 1:
            own_products(y, v.at[rows_of(c)])
            convert(r, v[:, cols_of(s)])
        if 2 <= k <= 4:
            i = k - 2
            y1[i].wait_recv()
            ysrc = lax.rem(y + 4 - (1, 3, 2)[i], 4)
            own_products(ysrc, x2o.at[ysrc])
        if k >= 4:
            lo_products(k - 4)
        if k >= 5:
            for i in {5: (0, 1, 2), 6: (3, 4), 7: (5, 6)}[k]:
                z1[i].wait_recv()
                b = xhi * 8 + frm[i]
                convert(b, x1f[b])
    for k in range(4, 8):
        lo_products(k)

    sends_d = []
    for j, (dy, dx) in enumerate(YX):
        cp = yx_to(dy, dx)
        dst = do.at[j] if j < 7 else dl.at[c]

        def block(q, _, cp=cp, dst=dst):
            row = cp * 16 + q
            acc = yd[dpats[row, 0], dcols[row, 0]]
            for h in range(1, HOPS):
                acc = acc + yd[dpats[row, h], dcols[row, h]]
            dst[q] = acc
            return 0

        lax.fori_loop(0, 16, block, 0)
        if j < 7:
            sends_d.append(go(remote(do.at[j], dl.at[c], d_s.at[j], d_r.at[j], (r, cp))))

    for k in range(7):
        z2[k].wait_recv()
        b = (1 - xhi) * 8 + frm[k]
        convert(b, x1f[b])
    relay_hi(7)
    convert(rhi, vh[s])

    sends_u = []
    for j in range(8):
        row = xhi * 8 + to[j]
        lhs = jnp.concatenate([phl[upats[row, h]] for h in range(HOPS)], axis=1)
        rhs = jnp.concatenate([x1h[ucols[row, h]] for h in range(HOPS)], axis=0)
        a = jnp.dot(lhs, rhs, preferred_element_type=f32)
        rhs = jnp.concatenate([x1l[ucols[row, h]] for h in range(HOPS)], axis=0)
        b = jnp.dot(lhs[0:BLK], rhs, preferred_element_type=f32)
        out = a[0:BLK] + a[BLK : 2 * BLK] + b
        if j < 7:
            uo[j] = out
            sends_u.append(go(remote(uo.at[j], ul.at[s], u_s.at[j], u_r.at[j], (xhi * 8 + to[j], c))))
        else:
            ul[s] = out

    for cp in sends_d:
        cp.wait_recv()
    locals_[5].wait()
    for cp in sends_u:
        cp.wait_recv()

    beta = beta_ref[0]

    def image(i, accs):
        vi, vw = accs
        rs = pl.ds(pl.multiple_of(i * 16, 16), 16)
        for j in range(16):
            cs = slice(j * BLK, (j + 1) * BLK)
            hs = slice((j % 2) * BLK, (j % 2) * BLK + BLK)
            im = ul[j // 2, rs, hs] + dl[i, j] + wbuf[rs, cs]
            w = im - beta * prev[rs, cs]
            wbuf[rs, cs] = w
            vv = v[rs, cs]
            vi = vi + vv * im
            vw = vw + vv * w
        return vi, vw

    zero = jnp.zeros((16, BLK), f32)
    vi, vw = lax.fori_loop(0, 8, image, (zero, zero))
    out_cp = pltpu.make_async_copy(wbuf, w_hbm, lsem.at[6])
    out_cp.start()
    sum_vi, sum_vw = total_of(vi), total_of(vw)
    a_loc = jnp.where(sum_vv > 0.0, sum_vw / jnp.where(sum_vv > 0.0, sum_vv, 1.0), 0.0)

    def rest(i, accs):
        rr, rv = accs
        rs = pl.ds(pl.multiple_of(i * 16, 16), 16)
        for j in range(16):
            cs = slice(j * BLK, (j + 1) * BLK)
            vv = v[rs, cs]
            res = wbuf[rs, cs] - a_loc * vv
            rr = rr + res * res
            rv = rv + res * vv
        return rr, rv

    rr, rv = lax.fori_loop(0, 8, rest, (zero, zero))
    stats = [sum_vi, sum_vv, total_of(rr), total_of(rv), a_loc]
    stats = [jnp.broadcast_to(x, (1, BLK)) for x in stats]

    def put(ref, idx, vals):
        for i, x in enumerate(vals):
            ref[idx, i : i + 1] = x

    def merge(ref, n):
        vis = sum(ref[i, 0:1] for i in range(n))
        vvs = sum(ref[i, 1:2] for i in range(n))
        vws = sum(ref[i, 4:5] * ref[i, 1:2] + ref[i, 3:4] for i in range(n))
        a = jnp.where(vvs > 0.0, vws / jnp.where(vvs > 0.0, vvs, 1.0), 0.0)
        rrs, rvs = 0.0, 0.0
        for i in range(n):
            d = a - ref[i, 4:5]
            rrs = rrs + (ref[i, 2:3] - 2.0 * d * ref[i, 3:4] + d * d * ref[i, 1:2])
            rvs = rvs + (ref[i, 3:4] - d * ref[i, 1:2])
        return [vis, vvs, rrs, rvs, a]

    def stage(ref, idx, devs, ss, rs):
        put(ref, idx, stats)
        cps = [go(remote(ref.at[idx], ref.at[idx], ss.at[i], rs.at[i], d)) for i, d in enumerate(devs)]
        for cp in cps:
            cp.wait_recv()
        return merge(ref, len(devs) + 1)

    stats = stage(g1, s, [(xhi * 8 + to[k], c) for k in range(7)], g1_s, g1_r)
    stats = stage(g2, c, [(r, yx_to(dy, dx)) for dy, dx in YX[:7]], g2_s, g2_r)
    stats = stage(g3, xhi, [dev_hi], g3_s, g3_r)
    vis, vvs, rrs, rvs, a = stats
    alpha = vis / vvs
    d = alpha - a
    energy = rrs - 2.0 * d * rvs + d * d * vvs
    scale = jnp.sqrt(energy / (2048 * 16384) + 1e-06)
    coef[...] = jnp.concatenate([alpha, scale, jnp.zeros((6, BLK), f32)], axis=0)
    for cp in started:
        cp.wait_send()
    out_cp.wait()


def local(
    vector, previous, beta_prev, hubbard_u, up_patterns, down_patterns,
    up_cols, up_pats, down_cols, down_pats, up_occupied, down_occupied,
):
    hbm = pl.BlockSpec(memory_space=pl.ANY)
    smem = pl.BlockSpec(memory_space=pltpu.SMEM)
    vmem = pl.BlockSpec(memory_space=pltpu.VMEM)
    dma = pltpu.SemaphoreType.DMA
    vm = pltpu.VMEM
    w, coef = pl.pallas_call(
        kernel,
        name="lanczos_step",
        out_shape=(
            jax.ShapeDtypeStruct((128, 2048), f32),
            jax.ShapeDtypeStruct((8, BLK), f32),
        ),
        in_specs=[hbm] * 6 + [smem] * 6,
        out_specs=(hbm, vmem),
        scratch_shapes=[
            vm((128, 2048), f32),
            vm((128, 2048), f32),
            vm((128, 2048), f32),
            vm((NPAT, BLK, BLK), f32),
            vm((NPAT, BLK, BLK), f32),
            vm((20, BLK), jnp.int32),
            vm((20, 2048), jnp.int32),
            vm((8, BLK, 256), f32),
            vm((8, BLK, 256), f32),
            vm((16, BLK, 256), f32),
            vm((16, BLK, 256), bf16),
            vm((16, BLK, 256), bf16),
            vm((4, 16, 2048), f32),
            vm((4, 8, 16, 256), f32),
            vm((NPAT, 3 * BLK, BLK), bf16),
            vm((NPAT, 2 * BLK, BLK), bf16),
            vm((NPAT, 128, 16, BLK), f32),
            vm((7, BLK, 256), f32),
            vm((7, 16, 16, BLK), f32),
            vm((8, BLK, 256), f32),
            vm((8, 16, 16, BLK), f32),
            vm((8, 8, BLK), f32),
            vm((8, 8, BLK), f32),
            vm((2, 8, BLK), f32),
            dma((7,)),
            dma((8,)), dma((8,)), dma((8,)), dma((8,)),
            dma((7,)), dma((7,)), dma((3,)), dma((3,)),
            dma((7,)), dma((7,)), dma((8, 3)), dma((8, 3)),
            dma((7,)), dma((7,)), dma((7,)), dma((7,)),
            dma((7,)), dma((7,)), dma((7,)), dma((7,)), dma((1,)), dma((1,)),
        ],
        compiler_params=pltpu.CompilerParams(
            collective_id=0, has_side_effects=True, vmem_limit_bytes=48 << 20
        ),
    )(
        vector, previous, up_patterns, down_patterns, up_occupied, down_occupied,
        beta_prev, hubbard_u, up_cols, up_pats, down_cols, down_pats,
    )
    alpha, scale = coef[0, 0], coef[1, 0]
    return ((w - alpha * vector) / scale, coef[0:2, 0])


def solution(mesh):
    in_specs = (
        P("row", "col"),
        P("row", "col"),
        P(),
        P(),
        P(),
        P(),
        P(),
        P(),
        P(),
        P(),
        P(None, "row"),
        P(None, "col"),
    )
    out_specs = (P("row", "col"), P())
    return jax.shard_map(local, mesh=mesh, in_specs=in_specs, out_specs=out_specs, check_vma=False)
```

```python
import jax
import jax.numpy as jnp
from jax import lax
from jax.experimental import pallas as pl
from jax.experimental.pallas import tpu as pltpu
from jax.sharding import PartitionSpec as P

MESH = pl.DeviceIdType.MESH
f32, bf16 = jnp.float32, jnp.bfloat16
BLK = 128
CID = 0
HOPS = 12
NPAT = 16
AHEAD = 4
EARLY = 3
ZC = [(1, 0), (3, 1), (2, 0), (1, 1), (3, 0), (2, 1), (0, 1), (0, 0)]
YX = [(1, 1), (3, 1), (2, 1), (1, 0), (0, 1), (3, 0), (2, 0), (0, 0)]


def split(x):
    hi = x.astype(bf16)
    lo = (x - hi.astype(f32)).astype(bf16)
    return hi, lo


def total_of(x):
    return jnp.sum(x, axis=(0, 1), keepdims=True)


def ratio(p, q):
    return jnp.where(q > 0.0, p / jnp.where(q > 0.0, q, 1.0), 0.0)


def kernel(
    v_hbm, prev_hbm, upat_hbm, dpat_hbm, upo_hbm, dno_hbm,
    beta_ref, hub_ref, ucols, upats, didx,
    out_hbm, coef,
    v, prev, wbuf, upat, dpat, upo, dno,
    vl, vh, x1f, x1h, x1l, x2o, x2p, dw, phl, yd,
    uo, do, ul, dl, g1, g2, g2s,
    lsem, osem, xl_s, xl_r, xh_s, xh_r, z1_s, z1_r, y1_s, y1_r, z2_s, z2_r, y2_s, y2_r,
    u_s, u_r, d_s, d_r, g1_s, g1_r, g2_s, g2_r,
):
    r, c = lax.axis_index("row"), lax.axis_index("col")
    xhi, s = lax.div(r, 8), lax.rem(r, 8)
    z, core = lax.div(s, 2), lax.rem(s, 2)
    y, xlo = lax.div(c, 2), lax.rem(c, 2)
    rhi = (1 - xhi) * 8 + s
    clo = y * 2 + 1 - xlo
    dev_lo, dev_x3 = (r, clo), (rhi, clo)

    def zc_to(k):
        dz, dc = ZC[k]
        return lax.rem(z + dz, 4) * 2 + lax.rem(core + dc, 2)

    def zc_from(k):
        dz, dc = ZC[k]
        return lax.rem(z + 4 - dz, 4) * 2 + lax.rem(core + 2 - dc, 2)

    def yx_to(dy, dx):
        return lax.rem(y + dy, 4) * 2 + lax.rem(xlo + dx, 2)

    def yx_from(dy, dx):
        return lax.rem(y + 4 - dy, 4) * 2 + lax.rem(xlo + 2 - dx, 2)

    def cols_of(k):
        return pl.ds(pl.multiple_of(k * 256, 256), 256)

    def rows_of(k):
        return pl.ds(pl.multiple_of(k * 16, 16), 16)

    def remote(src, dst, ssem, rsem, dev):
        return pltpu.make_async_remote_copy(
            src_ref=src, dst_ref=dst, send_sem=ssem, recv_sem=rsem, device_id=dev, device_id_type=MESH
        )

    locals_ = [
        pltpu.make_async_copy(a, b, lsem.at[i])
        for i, (a, b) in enumerate(
            [
                (v_hbm, v),
                (upat_hbm, upat),
                (dpat_hbm, dpat),
                (upo_hbm, upo),
                (dno_hbm, dno),
                (prev_hbm, prev),
            ]
        )
    ]
    barrier = pltpu.get_barrier_semaphore()
    peers = [(xhi * 8 + zc_to(k), c) for k in range(7)]
    peers += [(r, yx_to(dy, dx)) for dy, dx in YX[:7]]
    peers += [dev_x3]
    for dev in peers:
        pl.semaphore_signal(barrier, inc=1, device_id=dev, device_id_type=MESH)
    for cp in locals_:
        cp.start()
    pl.semaphore_wait(barrier, len(peers))

    started = []


    def go(cp):
        cp.start()
        started.append(cp)
        return cp

    to = [zc_to(k) for k in range(8)]
    frm = [zc_from(k) for k in range(8)]

    chunks = [(k, 0, BLK) for k in range(6)] + [(k, h, 64) for k in (6, 7) for h in (0, 64)]

    def send_x(i):
        k, h, n = chunks[i]
        rs = pl.ds(h, n)
        return go(remote(v_hbm.at[rs, cols_of(to[k])], vl.at[to[k], rs], xl_s.at[i], xl_r.at[i], dev_lo))

    xl = [send_x(i) for i in range(AHEAD)]
    z1, y1 = [], []
    for k in range(7):
        z1.append(
            go(remote(v_hbm.at[:, cols_of(to[k])], x1f.at[r], z1_s.at[k], z1_r.at[k], (xhi * 8 + to[k], c)))
        )
        if k < 3:
            dy = (1, 3, 2)[k]
            cp = yx_to(dy, 0)
            y1.append(go(remote(v_hbm.at[rows_of(cp)], x2o.at[y], y1_s.at[k], y1_r.at[k], (r, cp))))

    locals_[1].wait()
    locals_[2].wait()

    def prep(t, _):
        hi, lo = split(upat[t])
        phl[t, 0:BLK] = hi
        phl[t, BLK : 2 * BLK] = lo
        hi, lo = split(dpat[t].T)
        dw[t, 0:BLK] = hi
        dw[t, BLK : 2 * BLK] = hi
        dw[t, 2 * BLK : 3 * BLK] = lo
        return 0

    lax.fori_loop(0, NPAT, prep, 0)
    locals_[0].wait()

    def make_base():
        locals_[3].wait()
        locals_[4].wait()
        ups = upo[...].astype(f32).T
        hub = hub_ref[0]

        def step(i, acc):
            cs = pl.ds(pl.multiple_of(i * 256, 256), 256)
            both = jnp.dot(ups, dno[:, cs].astype(f32), preferred_element_type=f32)
            vv = v[:, cs]
            wbuf[:, cs] = hub * both * vv
            sq = vv * vv
            return acc + sum(sq[8 * a : 8 * a + 8] for a in range(16))

        acc = lax.fori_loop(0, 8, step, jnp.zeros((8, 256), f32))
        return total_of(acc)

    def products(xs, k0s, n):
        hi, lo = split(xs)
        lhs = jnp.concatenate([hi, lo, hi], axis=1)

        def step(i, _):
            rhs = jnp.concatenate([dw[i * 4 + a] for a in range(4)], axis=1)
            out = jnp.dot(lhs, rhs, preferred_element_type=f32)
            for a in range(4):
                for b, k0 in enumerate(k0s):
                    part = out[b * n * 16 : (b + 1) * n * 16, a * BLK : (a + 1) * BLK]
                    yd[pl.ds((i * 4 + a) * 128 + k0, n)] = part.reshape(n, 16, BLK)
            return 0

        lax.fori_loop(0, NPAT // 4, step, 0)

    def own_products(ysrc, ref):
        xs = jnp.concatenate([ref[:, j * BLK : (j + 1) * BLK] for j in range(16)], axis=0)
        products(xs, [(ysrc * 2 + xlo) * 16], 16)

    def lo_products(k):
        for i in range(3):
            y2[k][i].wait_recv()
        xs, k0s = [], []
        for dy in range(4):
            ysrc = lax.rem(y + 4 - dy, 4)
            if dy == 0:
                piece = vl[to[k], rows_of(c)]
            else:
                piece = x2p[ysrc, to[k]]
            xs += [piece[:, 0:BLK], piece[:, BLK : 2 * BLK]]
            k0s.append((ysrc * 2 + 1 - xlo) * 16 + to[k] * 2)
        products(jnp.concatenate(xs, axis=0), k0s, 2)

    def convert(b, x):
        hi, lo = split(x)
        x1h[b] = hi
        x1l[b] = lo

    xh, z2, y2 = [], [], []

    def relay_hi(i):
        k, h, n = chunks[i]
        xh[i].wait_recv()
        if h + n == BLK and k < 7:
            z2.append(go(remote(vh.at[to[k]], x1f.at[rhi], z2_s.at[k], z2_r.at[k], (xhi * 8 + to[k], c))))

    def hi_convert(k):
        if k < 7:
            z2[k].wait_recv()
            b = (1 - xhi) * 8 + frm[k]
            convert(b, x1f[b])
        else:
            convert(rhi, vh[s])

    def own_convert(i):
        z1[i].wait_recv()
        b = xhi * 8 + frm[i]
        convert(b, x1f[b])

    def y_job(i):
        y1[i].wait_recv()
        ysrc = lax.rem(y + 4 - (1, 3, 2)[i], 4)
        own_products(ysrc, x2o.at[ysrc])

    sends_d, sends_u = [], []

    def down_share(j):
        cp = yx_to(*YX[j])

        def block(q, _):
            for n in range(2):
                row = cp * 16 + q * 2 + n
                parts = []
                for i in range(HOPS):
                    parts.append(yd[didx[i, row]])
                while len(parts) > 1:
                    parts = [sum(parts[i : i + 2]) for i in range(0, len(parts), 2)]
                if j < 7:
                    do[j, q * 2 + n] = parts[0]
                else:
                    dl[c, q * 2 + n] = parts[0]
            return 0

        lax.fori_loop(0, 8, block, 0)
        if j < 7:
            sends_d.append(go(remote(do.at[j], dl.at[c], d_s.at[j], d_r.at[j], (r, cp))))

    def up_block(j):
        row = xhi * 8 + to[j]
        lhs = jnp.concatenate([phl[upats[row, h]] for h in range(HOPS)], axis=1)
        rhs = jnp.concatenate([x1h[ucols[row, h]] for h in range(HOPS)], axis=0)
        a = jnp.dot(lhs, rhs, preferred_element_type=f32)
        rhs = jnp.concatenate([x1l[ucols[row, h]] for h in range(HOPS)], axis=0)
        b = jnp.dot(lhs[0:BLK], rhs, preferred_element_type=f32)
        out = a[0:BLK] + a[BLK : 2 * BLK] + b
        if j < 7:
            uo[j] = out
            sends_u.append(go(remote(uo.at[j], ul.at[s], u_s.at[j], u_r.at[j], (xhi * 8 + to[j], c))))
        else:
            ul[s] = out

    jobs = {
        1: [lambda: y_job(0), lambda: y_job(1)],
        2: [lambda: y_job(2), lambda: lo_products(0)],
        3: [lambda: lo_products(1)] + [lambda i=i: own_convert(i) for i in range(3)],
        4: [lambda: lo_products(2)] + [lambda i=i: own_convert(i) for i in range(3, 7)],
        5: [lambda: lo_products(3), lambda: hi_convert(0), lambda: hi_convert(1)],
        6: [lambda: lo_products(4)],
        7: [lambda: hi_convert(2), lambda: hi_convert(3)],
        8: [lambda: lo_products(5)],
        9: [lambda: hi_convert(4)],
    }
    sum_vv = None
    for i, (k, h, n) in enumerate(chunks):
        rs = pl.ds(h, n)
        xl[i].wait_recv()
        if i + AHEAD < len(chunks):
            xl.append(send_x(i + AHEAD))
        xh.append(go(remote(vl.at[to[k], rs], vh.at[to[k], rs], xh_s.at[i], xh_r.at[i], dev_x3)))
        if h + n == BLK:
            row = []
            for m, dy in enumerate((1, 3, 2)):
                cp = yx_to(dy, 0)
                src = vl.at[to[k], rows_of(cp)]
                row.append(go(remote(src, x2p.at[y, to[k]], y2_s.at[k, m], y2_r.at[k, m], (r, cp))))
            y2.append(row)
        if i >= 1:
            relay_hi(i - 1)
        if i == 0:
            sum_vv = make_base()
            own_products(y, v.at[rows_of(c)])
            convert(r, v[:, cols_of(s)])
        for job in jobs.get(i, []):
            job()
    lo_products(6)
    lo_products(7)
    for j in range(EARLY):
        down_share(j)
    relay_hi(len(chunks) - 1)
    for k in range(5, 8):
        hi_convert(k)
    for j in range(8):
        up_block(j)
        if j + EARLY < 8:
            down_share(j + EARLY)

    for cp in sends_d:
        cp.wait_recv()
    locals_[5].wait()
    for cp in sends_u:
        cp.wait_recv()

    beta = beta_ref[0]

    def image(i, accs):
        vi, vw = accs
        rs = pl.ds(pl.multiple_of(i * 16, 16), 16)
        for j in range(16):
            cs = slice(j * BLK, (j + 1) * BLK)
            hs = slice((j % 2) * BLK, (j % 2) * BLK + BLK)
            im = ul[j // 2, rs, hs] + dl[i, j] + wbuf[rs, cs]
            w = im - beta * prev[rs, cs]
            wbuf[rs, cs] = w
            vv = v[rs, cs]
            vi = vi + vv * im
            vw = vw + vv * w
        return vi, vw

    zero = jnp.zeros((16, BLK), f32)
    vi, vw = lax.fori_loop(0, 8, image, (zero, zero))
    sum_vi, sum_vw = total_of(vi), total_of(vw)
    a_loc = ratio(sum_vw, sum_vv)

    def rest(i, accs):
        rr, rv = accs
        rs = pl.ds(pl.multiple_of(i * 16, 16), 16)
        for j in range(16):
            cs = slice(j * BLK, (j + 1) * BLK)
            vv = v[rs, cs]
            res = wbuf[rs, cs] - a_loc * vv
            rr = rr + res * res
            rv = rv + res * vv
        return rr, rv

    rr, rv = lax.fori_loop(0, 8, rest, (zero, zero))
    stats = [sum_vi, sum_vv, total_of(rr), total_of(rv), a_loc]
    lane = lax.broadcasted_iota(jnp.int32, (1, BLK), 1)

    def row_of(vals):
        row = jnp.zeros((1, BLK), f32)
        for i, x in enumerate(vals):
            row = jnp.where(lane == i, x, row)
        return row

    def merge(t):
        vis, vvs, rrs, rvs, a_s = [t[:, i : i + 1] for i in range(5)]

        def add(x):
            return jnp.sum(x, axis=0, keepdims=True)

        vv = add(vvs)
        a = ratio(add(a_s * vvs + rvs), vv)
        d = a - a_s
        return [add(vis), vv, add(rrs - 2.0 * d * rvs + d * d * vvs), add(rvs - d * vvs), a]

    g1[core] = row_of(stats)
    cp = go(remote(g1.at[core], g1.at[core], g1_s, g1_r, (xhi * 8 + z * 2 + 1 - core, c)))
    cp.wait_recv()
    stats = merge(jnp.concatenate([g1[0], g1[1]], axis=0))
    x = xhi * 2 + xlo
    chip = x * 16 + y * 4 + z
    g2[chip] = row_of(stats)

    def to_chip(i):
        xx = lax.rem(x + lax.div(i, 16), 4)
        yy = lax.rem(y + lax.rem(lax.div(i, 4), 4), 4)
        zz = lax.rem(z + lax.rem(i, 4), 4)
        dev = (lax.div(xx, 2) * 8 + zz * 2 + core, yy * 2 + lax.rem(xx, 2))
        return remote(g2.at[chip], g2.at[chip], g2_s.at[i], g2_r.at[i], dev)

    def all_chips(act):
        def body(i, _):
            act(to_chip(i))
            return 0

        lax.fori_loop(1, 64, body, 0)

    all_chips(lambda cp: cp.start())
    all_chips(lambda cp: cp.wait_recv())
    for i in range(64):
        g2s[i : i + 1] = g2[i]
    vis, vvs, rrs, rvs, a = merge(g2s[...])
    alpha = vis / vvs
    d = alpha - a
    energy = rrs - 2.0 * d * rvs + d * d * vvs
    scale = jnp.sqrt(energy / (2048 * 16384) + 1e-06)
    outs = []
    for i in range(4):
        rs = pl.ds(i * 32, 32)
        wbuf[rs] = (wbuf[rs] - alpha * v[rs]) / scale
        cp = pltpu.make_async_copy(wbuf.at[rs], out_hbm.at[rs], osem.at[i])
        cp.start()
        outs.append(cp)
    coef[0] = alpha[0, 0]
    coef[1] = scale[0, 0]
    all_chips(lambda cp: cp.wait_send())
    for cp in started:
        cp.wait_send()
    for cp in outs:
        cp.wait()


def local(
    vector, previous, beta_prev, hubbard_u, up_patterns, down_patterns,
    up_cols, up_pats, down_cols, down_pats, up_occupied, down_occupied,
):
    hbm = pl.BlockSpec(memory_space=pl.ANY)
    smem = pl.BlockSpec(memory_space=pltpu.SMEM)
    dma = pltpu.SemaphoreType.DMA
    vm = pltpu.VMEM
    return pl.pallas_call(
        kernel,
        name="lanczos_step",
        out_shape=(
            jax.ShapeDtypeStruct((128, 2048), f32),
            jax.ShapeDtypeStruct((2,), f32),
        ),
        in_specs=[hbm] * 6 + [smem] * 5,
        out_specs=(hbm, smem),
        scratch_shapes=[
            vm((128, 2048), f32),
            vm((128, 2048), f32),
            vm((128, 2048), f32),
            vm((NPAT, BLK, BLK), f32),
            vm((NPAT, BLK, BLK), f32),
            vm((20, BLK), jnp.int32),
            vm((20, 2048), jnp.int32),
            vm((8, BLK, 256), f32),
            vm((8, BLK, 256), f32),
            vm((16, BLK, 256), f32),
            vm((16, BLK, 256), bf16),
            vm((16, BLK, 256), bf16),
            vm((4, 16, 2048), f32),
            vm((4, 8, 16, 256), f32),
            vm((NPAT, 3 * BLK, BLK), bf16),
            vm((NPAT, 2 * BLK, BLK), bf16),
            vm((NPAT * 128, 16, BLK), f32),
            vm((7, BLK, 256), f32),
            vm((7, 16, 16, BLK), f32),
            vm((8, BLK, 256), f32),
            vm((8, 16, 16, BLK), f32),
            vm((2, 1, BLK), f32),
            vm((64, 1, BLK), f32),
            vm((64, BLK), f32),
            dma((6,)), dma((4,)),
            dma((10,)), dma((10,)), dma((10,)), dma((10,)),
            dma((7,)), dma((7,)), dma((3,)), dma((3,)),
            dma((7,)), dma((7,)), dma((8, 3)), dma((8, 3)),
            dma((7,)), dma((7,)), dma((7,)), dma((7,)),
            dma, dma, dma((64,)), dma((64,)),
        ],
        compiler_params=pltpu.CompilerParams(
            collective_id=CID, has_side_effects=True, vmem_limit_bytes=60 << 20
        ),
    )(
        vector, previous, up_patterns, down_patterns, up_occupied, down_occupied,
        beta_prev, hubbard_u, up_cols, up_pats, (down_pats * 128 + down_cols).T,
    )


def solution(mesh):
    in_specs = (
        P("row", "col"),
        P("row", "col"),
        P(),
        P(),
        P(),
        P(),
        P(),
        P(),
        P(),
        P(),
        P(None, "row"),
        P(None, "col"),
    )
    out_specs = (P("row", "col"), P())
    return jax.shard_map(local, mesh=mesh, in_specs=in_specs, out_specs=out_specs, check_vma=False)
```

```python
import jax
import jax.numpy as jnp
from jax import lax
from jax.experimental import pallas as pl
from jax.experimental.pallas import tpu as pltpu
from jax.sharding import PartitionSpec as P

MESH = pl.DeviceIdType.MESH
f32, bf16 = jnp.float32, jnp.bfloat16
BLK = 128
CID = 0
HOPS = 12
NPAT = 16
AHEAD = 10
EARLY = 3
ZC = [(1, 0), (3, 1), (2, 0), (1, 1), (3, 0), (2, 1), (0, 1), (0, 0)]
YX = [(1, 1), (3, 1), (2, 1), (1, 0), (0, 1), (3, 0), (2, 0), (0, 0)]


def split(x):
    hi = x.astype(bf16)
    lo = (x - hi.astype(f32)).astype(bf16)
    return hi, lo


def total_of(x):
    return jnp.sum(x, axis=(0, 1), keepdims=True)


def ratio(p, q):
    return jnp.where(q > 0.0, p / jnp.where(q > 0.0, q, 1.0), 0.0)


def kernel(
    v_hbm, prev_hbm, upat_hbm, dpat_hbm, upo_hbm, dno_hbm,
    beta_ref, hub_ref, ucols, upats, dcols, dpats,
    out_hbm, coef,
    v, prev, wbuf, upat, dpat, upo, dno,
    vl, vh, x1f, x1h, x1l, x2o, x2p, dw, phl, yd,
    uo, do, ul, dl, g1, g2, g2s,
    lsem, osem, xl_s, xl_r, xh_s, xh_r, z1_s, z1_r, y1_s, y1_r, z2_s, z2_r, y2_s, y2_r,
    u_s, u_r, d_s, d_r, g1_s, g1_r, g2_s, g2_r,
):
    r, c = lax.axis_index("row"), lax.axis_index("col")
    xhi, s = lax.div(r, 8), lax.rem(r, 8)
    z, core = lax.div(s, 2), lax.rem(s, 2)
    y, xlo = lax.div(c, 2), lax.rem(c, 2)
    rhi = (1 - xhi) * 8 + s
    clo = y * 2 + 1 - xlo
    dev_lo, dev_x3 = (r, clo), (rhi, clo)

    def zc_to(k):
        dz, dc = ZC[k]
        return lax.rem(z + dz, 4) * 2 + lax.rem(core + dc, 2)

    def zc_from(k):
        dz, dc = ZC[k]
        return lax.rem(z + 4 - dz, 4) * 2 + lax.rem(core + 2 - dc, 2)

    def yx_to(dy, dx):
        return lax.rem(y + dy, 4) * 2 + lax.rem(xlo + dx, 2)

    def yx_from(dy, dx):
        return lax.rem(y + 4 - dy, 4) * 2 + lax.rem(xlo + 2 - dx, 2)

    def cols_of(k):
        return pl.ds(pl.multiple_of(k * 256, 256), 256)

    def rows_of(k):
        return pl.ds(pl.multiple_of(k * 16, 16), 16)

    def remote(src, dst, ssem, rsem, dev):
        return pltpu.make_async_remote_copy(
            src_ref=src, dst_ref=dst, send_sem=ssem, recv_sem=rsem, device_id=dev, device_id_type=MESH
        )

    locals_ = [
        pltpu.make_async_copy(a, b, lsem.at[i])
        for i, (a, b) in enumerate(
            [
                (v_hbm, v),
                (upat_hbm, upat),
                (dpat_hbm, dpat),
                (upo_hbm, upo),
                (dno_hbm, dno),
                (prev_hbm, prev),
            ]
        )
    ]
    barrier = pltpu.get_barrier_semaphore()
    peers = [(xhi * 8 + zc_to(k), c) for k in range(7)]
    peers += [(r, yx_to(dy, dx)) for dy, dx in YX[:7]]
    peers += [dev_x3]
    for dev in peers:
        pl.semaphore_signal(barrier, inc=1, device_id=dev, device_id_type=MESH)
    for cp in locals_:
        cp.start()
    pl.semaphore_wait(barrier, len(peers))

    started = []


    def go(cp):
        cp.start()
        started.append(cp)
        return cp

    to = [zc_to(k) for k in range(8)]
    frm = [zc_from(k) for k in range(8)]

    chunks = [(k, 0, BLK) for k in range(6)] + [(k, h, 64) for k in (6, 7) for h in (0, 64)]

    def send_x(i):
        k, h, n = chunks[i]
        rs = pl.ds(h, n)
        return go(remote(v_hbm.at[rs, cols_of(to[k])], vl.at[to[k], rs], xl_s.at[i], xl_r.at[i], dev_lo))

    xl = [send_x(i) for i in range(AHEAD)]
    z1, y1 = [], []
    for k in range(7):
        z1.append(
            go(remote(v_hbm.at[:, cols_of(to[k])], x1f.at[r], z1_s.at[k], z1_r.at[k], (xhi * 8 + to[k], c)))
        )
        if k < 3:
            dy = (1, 3, 2)[k]
            cp = yx_to(dy, 0)
            y1.append(go(remote(v_hbm.at[rows_of(cp)], x2o.at[y], y1_s.at[k], y1_r.at[k], (r, cp))))

    locals_[1].wait()
    locals_[2].wait()

    def prep(t, _):
        hi, lo = split(upat[t])
        phl[t, 0:BLK] = hi
        phl[t, BLK : 2 * BLK] = lo
        hi, lo = split(dpat[t].T)
        dw[t, 0:BLK] = hi
        dw[t, BLK : 2 * BLK] = hi
        dw[t, 2 * BLK : 3 * BLK] = lo
        return 0

    lax.fori_loop(0, NPAT, prep, 0)
    locals_[0].wait()

    def make_base():
        locals_[3].wait()
        locals_[4].wait()
        ups = upo[...].astype(f32).T
        hub = hub_ref[0]

        def step(i, acc):
            cs = pl.ds(pl.multiple_of(i * 256, 256), 256)
            both = jnp.dot(ups, dno[:, cs].astype(f32), preferred_element_type=f32)
            vv = v[:, cs]
            wbuf[:, cs] = hub * both * vv
            sq = vv * vv
            return acc + sum(sq[8 * a : 8 * a + 8] for a in range(16))

        acc = lax.fori_loop(0, 8, step, jnp.zeros((8, 256), f32))
        return total_of(acc)

    def products(xs, k0s, n):
        hi, lo = split(xs)
        lhs = jnp.concatenate([hi, lo, hi], axis=1)

        def step(i, _):
            rhs = jnp.concatenate([dw[i * 4 + a] for a in range(4)], axis=1)
            out = jnp.dot(lhs, rhs, preferred_element_type=f32)
            for a in range(4):
                for b, k0 in enumerate(k0s):
                    part = out[b * n * 16 : (b + 1) * n * 16, a * BLK : (a + 1) * BLK]
                    yd[pl.ds((i * 4 + a) * 128 + k0, n)] = part.reshape(n, 16, BLK)
            return 0

        lax.fori_loop(0, NPAT // 4, step, 0)

    def own_products(ysrc, ref):
        xs = jnp.concatenate([ref[:, j * BLK : (j + 1) * BLK] for j in range(16)], axis=0)
        products(xs, [(ysrc * 2 + xlo) * 16], 16)

    def lo_products(*ks):
        xs, k0s = [], []
        for k in ks:
            for i in range(3):
                y2[k][i].wait_recv()
            for dy in range(4):
                ysrc = lax.rem(y + 4 - dy, 4)
                if dy == 0:
                    piece = vl[to[k], rows_of(c)]
                else:
                    piece = x2p[ysrc, to[k]]
                xs += [piece[:, 0:BLK], piece[:, BLK : 2 * BLK]]
                k0s.append((ysrc * 2 + 1 - xlo) * 16 + to[k] * 2)
        products(jnp.concatenate(xs, axis=0), k0s, 2)

    def convert(b, x):
        hi, lo = split(x)
        x1h[b] = hi
        x1l[b] = lo

    xh, z2, y2 = [], [], []

    def relay_hi(i):
        k, h, n = chunks[i]
        xh[i].wait_recv()
        if h + n == BLK and k < 7:
            z2.append(go(remote(vh.at[to[k]], x1f.at[rhi], z2_s.at[k], z2_r.at[k], (xhi * 8 + to[k], c))))

    def hi_convert(k):
        if k < 7:
            z2[k].wait_recv()
            b = (1 - xhi) * 8 + frm[k]
            convert(b, x1f[b])
        else:
            convert(rhi, vh[s])

    def own_convert(i):
        z1[i].wait_recv()
        b = xhi * 8 + frm[i]
        convert(b, x1f[b])

    def y_job(i):
        y1[i].wait_recv()
        ysrc = lax.rem(y + 4 - (1, 3, 2)[i], 4)
        own_products(ysrc, x2o.at[ysrc])

    sends_d, sends_u = [], []

    def down_share(j):
        cp = yx_to(*YX[j])

        def block(q, _):
            for n in range(2):
                row = cp * 16 + q * 2 + n
                parts = []
                for i in range(HOPS):
                    parts.append(yd[dpats[i, row] * 128 + dcols[i, row]])
                while len(parts) > 1:
                    parts = [sum(parts[i : i + 2]) for i in range(0, len(parts), 2)]
                if j < 7:
                    do[j, q * 2 + n] = parts[0]
                else:
                    dl[c, q * 2 + n] = parts[0]
            return 0

        lax.fori_loop(0, 8, block, 0)
        if j < 7:
            sends_d.append(go(remote(do.at[j], dl.at[c], d_s.at[j], d_r.at[j], (r, cp))))

    def up_block(j):
        row = xhi * 8 + to[j]
        lhs = jnp.concatenate([phl[upats[row, h]] for h in range(HOPS)], axis=1)
        rhs = jnp.concatenate([x1h[ucols[row, h]] for h in range(HOPS)], axis=0)
        a = jnp.dot(lhs, rhs, preferred_element_type=f32)
        rhs = jnp.concatenate([x1l[ucols[row, h]] for h in range(HOPS)], axis=0)
        b = jnp.dot(lhs[0:BLK], rhs, preferred_element_type=f32)
        out = a[0:BLK] + a[BLK : 2 * BLK] + b
        if j < 7:
            uo[j] = out
            sends_u.append(go(remote(uo.at[j], ul.at[s], u_s.at[j], u_r.at[j], (xhi * 8 + to[j], c))))
        else:
            ul[s] = out

    jobs = {
        1: [lambda: y_job(0), lambda: y_job(1)],
        2: [lambda: y_job(2)],
        3: [lambda: lo_products(0, 1)] + [lambda i=i: own_convert(i) for i in range(3)],
        4: [lambda i=i: own_convert(i) for i in range(3, 7)],
        5: [lambda: lo_products(2, 3), lambda: hi_convert(0), lambda: hi_convert(1)],
        7: [lambda: hi_convert(2), lambda: hi_convert(3)],
        9: [lambda: hi_convert(4)],
    }
    sum_vv = None
    for i, (k, h, n) in enumerate(chunks):
        rs = pl.ds(h, n)
        xl[i].wait_recv()
        if i + AHEAD < len(chunks):
            xl.append(send_x(i + AHEAD))
        xh.append(go(remote(vl.at[to[k], rs], vh.at[to[k], rs], xh_s.at[i], xh_r.at[i], dev_x3)))
        if h + n == BLK:
            row = []
            for m, dy in enumerate((1, 3, 2)):
                cp = yx_to(dy, 0)
                src = vl.at[to[k], rows_of(cp)]
                row.append(go(remote(src, x2p.at[y, to[k]], y2_s.at[k, m], y2_r.at[k, m], (r, cp))))
            y2.append(row)
        if i >= 1:
            relay_hi(i - 1)
        if i == 0:
            sum_vv = make_base()
            own_products(y, v.at[rows_of(c)])
            convert(r, v[:, cols_of(s)])
        for job in jobs.get(i, []):
            job()
    lo_products(4, 5)
    lo_products(6, 7)
    for j in range(EARLY):
        down_share(j)
    relay_hi(len(chunks) - 1)
    for k in range(5, 8):
        hi_convert(k)
    for j in range(8):
        up_block(j)
        if j + EARLY < 8:
            down_share(j + EARLY)

    for cp in sends_d:
        cp.wait_recv()
    locals_[5].wait()
    beta = beta_ref[0]
    zero = jnp.zeros((16, BLK), f32)
    vi, vw = zero, zero
    for k in (7, 0, 1, 2, 3, 4, 5, 6):
        if k < 7:
            sends_u[k].wait_recv()
        place = frm[k]

        def image(i, accs, place=place):
            vi, vw = accs
            rs = rows_of(i)
            for n in range(2):
                cs = pl.ds(pl.multiple_of(place * 256 + n * BLK, BLK), BLK)
                im = ul[place, rs, n * BLK : (n + 1) * BLK] + dl[i, place * 2 + n] + wbuf[rs, cs]
                w = im - beta * prev[rs, cs]
                wbuf[rs, cs] = w
                vv = v[rs, cs]
                vi = vi + vv * im
                vw = vw + vv * w
            return vi, vw

        vi, vw = lax.fori_loop(0, 8, image, (vi, vw))
    out_cp = pltpu.make_async_copy(wbuf, out_hbm, osem)
    out_cp.start()
    sum_vi, sum_vw = total_of(vi), total_of(vw)
    a_loc = ratio(sum_vw, sum_vv)

    def rest(i, accs):
        rr, rv = accs
        rs = pl.ds(pl.multiple_of(i * 16, 16), 16)
        for j in range(16):
            cs = slice(j * BLK, (j + 1) * BLK)
            vv = v[rs, cs]
            res = wbuf[rs, cs] - a_loc * vv
            rr = rr + res * res
            rv = rv + res * vv
        return rr, rv

    rr, rv = lax.fori_loop(0, 8, rest, (zero, zero))
    stats = [sum_vi, sum_vv, total_of(rr), total_of(rv), a_loc]
    lane = lax.broadcasted_iota(jnp.int32, (1, BLK), 1)

    def row_of(vals):
        row = jnp.zeros((1, BLK), f32)
        for i, x in enumerate(vals):
            row = jnp.where(lane == i, x, row)
        return row

    def merge(t):
        vis, vvs, rrs, rvs, a_s = [t[:, i : i + 1] for i in range(5)]

        def add(x):
            return jnp.sum(x, axis=0, keepdims=True)

        vv = add(vvs)
        a = ratio(add(a_s * vvs + rvs), vv)
        d = a - a_s
        return [add(vis), vv, add(rrs - 2.0 * d * rvs + d * d * vvs), add(rvs - d * vvs), a]

    g1[core] = row_of(stats)
    cp = go(remote(g1.at[core], g1.at[core], g1_s, g1_r, (xhi * 8 + z * 2 + 1 - core, c)))
    cp.wait_recv()
    stats = merge(jnp.concatenate([g1[0], g1[1]], axis=0))
    x = xhi * 2 + xlo
    chip = x * 16 + y * 4 + z
    g2[chip] = row_of(stats)

    def all_chips(act):
        def body(i, _):
            xx = lax.rem(x + lax.div(i, 4), 4)
            yy = lax.rem(y + lax.rem(i, 4), 4)
            base, col = lax.div(xx, 2) * 8 + core, yy * 2 + lax.rem(xx, 2)
            for n in range(4):
                dev = (base + lax.rem(z + n, 4) * 2, col)
                cp = remote(g2.at[chip], g2.at[chip], g2_s.at[i * 4 + n], g2_r.at[i * 4 + n], dev)
                if n > 0:
                    act(cp)
                else:
                    pl.when(i > 0)(lambda cp=cp: act(cp))
            return 0

        lax.fori_loop(0, 16, body, 0)

    all_chips(lambda cp: cp.start())
    all_chips(lambda cp: cp.wait_recv())
    for i in range(64):
        g2s[i : i + 1] = g2[i]
    vis, vvs, rrs, rvs, a = merge(g2s[...])
    alpha = vis / vvs
    d = alpha - a
    energy = rrs - 2.0 * d * rvs + d * d * vvs
    scale = jnp.sqrt(energy / (2048 * 16384) + 1e-06)
    coef[0] = alpha[0, 0]
    coef[1] = scale[0, 0]
    all_chips(lambda cp: cp.wait_send())
    for cp in started:
        cp.wait_send()
    out_cp.wait()


def finish(w_hbm, v_hbm, coef, out_hbm, coef_out, w, v, sem):
    parts = [pl.ds(i * 32, 32) for i in range(4)]
    ins = [
        [pltpu.make_async_copy(a.at[rs], b.at[rs], sem.at[n, i]) for n, (a, b) in enumerate(((w_hbm, w), (v_hbm, v)))]
        for i, rs in enumerate(parts)
    ]
    for pair in ins:
        for cp in pair:
            cp.start()
    alpha, scale = coef[0], coef[1]
    coef_out[0] = alpha
    coef_out[1] = scale
    outs = []
    for i, rs in enumerate(parts):
        for cp in ins[i]:
            cp.wait()
        w[rs] = (w[rs] - alpha * v[rs]) / scale
        outs.append(pltpu.make_async_copy(w.at[rs], out_hbm.at[rs], sem.at[2, i]))
        outs[i].start()
    for cp in outs:
        cp.wait()


def local(
    vector, previous, beta_prev, hubbard_u, up_patterns, down_patterns,
    up_cols, up_pats, down_cols, down_pats, up_occupied, down_occupied,
):
    hbm = pl.BlockSpec(memory_space=pl.ANY)
    smem = pl.BlockSpec(memory_space=pltpu.SMEM)
    dma = pltpu.SemaphoreType.DMA
    vm = pltpu.VMEM
    w, coef = pl.pallas_call(
        kernel,
        name="lanczos_step",
        out_shape=(
            jax.ShapeDtypeStruct((128, 2048), f32),
            jax.ShapeDtypeStruct((2,), f32),
        ),
        in_specs=[hbm] * 6 + [smem] * 6,
        out_specs=(hbm, smem),
        scratch_shapes=[
            vm((128, 2048), f32),
            vm((128, 2048), f32),
            vm((128, 2048), f32),
            vm((NPAT, BLK, BLK), f32),
            vm((NPAT, BLK, BLK), f32),
            vm((20, BLK), jnp.int32),
            vm((20, 2048), jnp.int32),
            vm((8, BLK, 256), f32),
            vm((8, BLK, 256), f32),
            vm((16, BLK, 256), f32),
            vm((16, BLK, 256), bf16),
            vm((16, BLK, 256), bf16),
            vm((4, 16, 2048), f32),
            vm((4, 8, 16, 256), f32),
            vm((NPAT, 3 * BLK, BLK), bf16),
            vm((NPAT, 2 * BLK, BLK), bf16),
            vm((NPAT * 128, 16, BLK), f32),
            vm((7, BLK, 256), f32),
            vm((7, 16, 16, BLK), f32),
            vm((8, BLK, 256), f32),
            vm((8, 16, 16, BLK), f32),
            vm((2, 1, BLK), f32),
            vm((64, 1, BLK), f32),
            vm((64, BLK), f32),
            dma((6,)), dma,
            dma((10,)), dma((10,)), dma((10,)), dma((10,)),
            dma((7,)), dma((7,)), dma((3,)), dma((3,)),
            dma((7,)), dma((7,)), dma((8, 3)), dma((8, 3)),
            dma((7,)), dma((7,)), dma((7,)), dma((7,)),
            dma, dma, dma((64,)), dma((64,)),
        ],
        compiler_params=pltpu.CompilerParams(
            collective_id=CID, has_side_effects=True, vmem_limit_bytes=60 << 20
        ),
    )(
        vector, previous, up_patterns, down_patterns, up_occupied, down_occupied,
        beta_prev, hubbard_u, up_cols, up_pats, down_cols.T, down_pats.T,
    )
    return pl.pallas_call(
        finish,
        name="scale_residual",
        out_shape=(
            jax.ShapeDtypeStruct((128, 2048), f32),
            jax.ShapeDtypeStruct((2,), f32),
        ),
        in_specs=[hbm, hbm, smem],
        out_specs=(hbm, smem),
        scratch_shapes=[vm((128, 2048), f32), vm((128, 2048), f32), dma((3, 4))],
        compiler_params=pltpu.CompilerParams(vmem_limit_bytes=60 << 20),
    )(w, vector, coef)


def solution(mesh):
    in_specs = (
        P("row", "col"),
        P("row", "col"),
        P(),
        P(),
        P(),
        P(),
        P(),
        P(),
        P(),
        P(),
        P(None, "row"),
        P(None, "col"),
    )
    out_specs = (P("row", "col"), P())
    return jax.shard_map(local, mesh=mesh, in_specs=in_specs, out_specs=out_specs, check_vma=False)
```

```python
import jax
import jax.numpy as jnp
from jax import lax
from jax.experimental import pallas as pl
from jax.experimental.pallas import tpu as pltpu
from jax.sharding import PartitionSpec as P

MESH = pl.DeviceIdType.MESH
f32, bf16 = jnp.float32, jnp.bfloat16
BLK = 128
CID = 0
HOPS = 12
NPAT = 16
AHEAD = 10
EARLY = 3
ZC = [(1, 0), (3, 1), (2, 0), (1, 1), (3, 0), (2, 1), (0, 1), (0, 0)]
YX = [(1, 1), (3, 1), (2, 1), (1, 0), (0, 1), (3, 0), (2, 0), (0, 0)]


def split(x):
    hi = x.astype(bf16)
    lo = (x - hi.astype(f32)).astype(bf16)
    return hi, lo


def total_of(x):
    return jnp.sum(x, axis=(0, 1), keepdims=True)


def ratio(p, q):
    return jnp.where(q > 0.0, p / jnp.where(q > 0.0, q, 1.0), 0.0)


def kernel(
    v_hbm, prev_hbm, upat_hbm, dpat_hbm, upo_hbm, dno_hbm,
    beta_ref, hub_ref, ucols, upats, dcols, dpats,
    out_hbm, coef,
    v, prev, wbuf, upat, dpat, upo, dno,
    vl, vh, x1f, x1h, x1l, x2o, x2p, dw, phl, yd,
    uo, do, ul, dl, g1, g2, g2s,
    lsem, osem, xl_s, xl_r, xh_s, xh_r, z1_s, z1_r, y1_s, y1_r, z2_s, z2_r, y2_s, y2_r,
    u_s, u_r, d_s, d_r, g1_s, g1_r, g2_s, g2_r,
):
    r, c = lax.axis_index("row"), lax.axis_index("col")
    xhi, s = lax.div(r, 8), lax.rem(r, 8)
    z, core = lax.div(s, 2), lax.rem(s, 2)
    y, xlo = lax.div(c, 2), lax.rem(c, 2)
    rhi = (1 - xhi) * 8 + s
    clo = y * 2 + 1 - xlo
    dev_lo, dev_x3 = (r, clo), (rhi, clo)

    def zc_to(k):
        dz, dc = ZC[k]
        return lax.rem(z + dz, 4) * 2 + lax.rem(core + dc, 2)

    def zc_from(k):
        dz, dc = ZC[k]
        return lax.rem(z + 4 - dz, 4) * 2 + lax.rem(core + 2 - dc, 2)

    def yx_to(dy, dx):
        return lax.rem(y + dy, 4) * 2 + lax.rem(xlo + dx, 2)

    def yx_from(dy, dx):
        return lax.rem(y + 4 - dy, 4) * 2 + lax.rem(xlo + 2 - dx, 2)

    def cols_of(k):
        return pl.ds(pl.multiple_of(k * 256, 256), 256)

    def rows_of(k):
        return pl.ds(pl.multiple_of(k * 16, 16), 16)

    def remote(src, dst, ssem, rsem, dev):
        return pltpu.make_async_remote_copy(
            src_ref=src, dst_ref=dst, send_sem=ssem, recv_sem=rsem, device_id=dev, device_id_type=MESH
        )

    locals_ = [
        pltpu.make_async_copy(a, b, lsem.at[i])
        for i, (a, b) in enumerate(
            [
                (v_hbm, v),
                (upat_hbm, upat),
                (dpat_hbm, dpat),
                (upo_hbm, upo),
                (dno_hbm, dno),
                (prev_hbm, prev),
            ]
        )
    ]
    barrier = pltpu.get_barrier_semaphore()
    peers = [(xhi * 8 + zc_to(k), c) for k in range(7)]
    peers += [(r, yx_to(dy, dx)) for dy, dx in YX[:7]]
    peers += [dev_x3]
    for dev in peers:
        pl.semaphore_signal(barrier, inc=1, device_id=dev, device_id_type=MESH)
    for cp in locals_[:5]:
        cp.start()
    pl.semaphore_wait(barrier, len(peers))

    started = []


    def go(cp):
        cp.start()
        started.append(cp)
        return cp

    to = [zc_to(k) for k in range(8)]
    frm = [zc_from(k) for k in range(8)]

    chunks = [(k, 0, BLK) for k in range(6)] + [(k, h, 64) for k in (6, 7) for h in (0, 64)]

    def send_x(i):
        k, h, n = chunks[i]
        rs = pl.ds(h, n)
        return go(remote(v_hbm.at[rs, cols_of(to[k])], vl.at[to[k], rs], xl_s.at[i], xl_r.at[i], dev_lo))

    xl = [send_x(i) for i in range(AHEAD)]
    z1, y1 = [], []
    for k in range(7):
        z1.append(
            go(remote(v_hbm.at[:, cols_of(to[k])], x1f.at[r], z1_s.at[k], z1_r.at[k], (xhi * 8 + to[k], c)))
        )
        if k < 3:
            dy = (1, 3, 2)[k]
            cp = yx_to(dy, 0)
            y1.append(go(remote(v_hbm.at[rows_of(cp)], x2o.at[y], y1_s.at[k], y1_r.at[k], (r, cp))))

    locals_[1].wait()
    locals_[2].wait()

    def prep(t, _):
        hi, lo = split(upat[t])
        phl[t, 0:BLK] = hi
        phl[t, BLK : 2 * BLK] = lo
        hi, lo = split(dpat[t].T)
        dw[t, 0:BLK] = hi
        dw[t, BLK : 2 * BLK] = hi
        dw[t, 2 * BLK : 3 * BLK] = lo
        return 0

    lax.fori_loop(0, NPAT, prep, 0)
    locals_[0].wait()

    def make_base():
        locals_[3].wait()
        locals_[4].wait()
        ups = upo[...].astype(f32).T
        hub = hub_ref[0]

        def step(i, acc):
            cs = pl.ds(pl.multiple_of(i * 256, 256), 256)
            both = jnp.dot(ups, dno[:, cs].astype(f32), preferred_element_type=f32)
            vv = v[:, cs]
            wbuf[:, cs] = hub * both * vv
            sq = vv * vv
            return acc + sum(sq[8 * a : 8 * a + 8] for a in range(16))

        acc = lax.fori_loop(0, 8, step, jnp.zeros((8, 256), f32))
        return total_of(acc)

    def products(xs, k0s, n):
        hi, lo = split(xs)
        lhs = jnp.concatenate([hi, lo, hi], axis=1)

        def step(i, _):
            rhs = jnp.concatenate([dw[i * 4 + a] for a in range(4)], axis=1)
            out = jnp.dot(lhs, rhs, preferred_element_type=f32)
            for a in range(4):
                for b, k0 in enumerate(k0s):
                    part = out[b * n * 16 : (b + 1) * n * 16, a * BLK : (a + 1) * BLK]
                    yd[pl.ds((i * 4 + a) * 128 + k0, n)] = part.reshape(n, 16, BLK)
            return 0

        lax.fori_loop(0, NPAT // 4, step, 0)

    def own_products(ysrc, ref):
        xs = jnp.concatenate([ref[:, j * BLK : (j + 1) * BLK] for j in range(16)], axis=0)
        products(xs, [(ysrc * 2 + xlo) * 16], 16)

    def lo_products(*ks):
        xs, k0s = [], []
        for k in ks:
            for i in range(3):
                y2[k][i].wait_recv()
            for dy in range(4):
                ysrc = lax.rem(y + 4 - dy, 4)
                if dy == 0:
                    piece = vl[to[k], rows_of(c)]
                else:
                    piece = x2p[ysrc, to[k]]
                xs += [piece[:, 0:BLK], piece[:, BLK : 2 * BLK]]
                k0s.append((ysrc * 2 + 1 - xlo) * 16 + to[k] * 2)
        products(jnp.concatenate(xs, axis=0), k0s, 2)

    def convert(b, x):
        hi, lo = split(x)
        x1h[b] = hi
        x1l[b] = lo

    xh, z2, y2 = [], [], []

    def relay_hi(i):
        k, h, n = chunks[i]
        xh[i].wait_recv()
        if h + n == BLK and k < 7:
            z2.append(go(remote(vh.at[to[k]], x1f.at[rhi], z2_s.at[k], z2_r.at[k], (xhi * 8 + to[k], c))))

    def hi_convert(k):
        if k < 7:
            z2[k].wait_recv()
            b = (1 - xhi) * 8 + frm[k]
            convert(b, x1f[b])
        else:
            convert(rhi, vh[s])

    def own_convert(i):
        z1[i].wait_recv()
        b = xhi * 8 + frm[i]
        convert(b, x1f[b])

    def y_job(i):
        y1[i].wait_recv()
        ysrc = lax.rem(y + 4 - (1, 3, 2)[i], 4)
        own_products(ysrc, x2o.at[ysrc])

    sends_d, sends_u = [], []

    def down_share(j):
        cp = yx_to(*YX[j])

        def block(q, _):
            for n in range(2):
                row = cp * 16 + q * 2 + n
                parts = []
                for i in range(HOPS):
                    parts.append(yd[dpats[i, row] * 128 + dcols[i, row]])
                while len(parts) > 1:
                    parts = [sum(parts[i : i + 2]) for i in range(0, len(parts), 2)]
                if j < 7:
                    do[j, q * 2 + n] = parts[0]
                else:
                    dl[c, q * 2 + n] = parts[0]
            return 0

        lax.fori_loop(0, 8, block, 0)
        if j < 7:
            sends_d.append(go(remote(do.at[j], dl.at[c], d_s.at[j], d_r.at[j], (r, cp))))

    def up_block(j):
        row = xhi * 8 + to[j]
        lhs = jnp.concatenate([phl[upats[row, h]] for h in range(HOPS)], axis=1)
        rhs = jnp.concatenate([x1h[ucols[row, h]] for h in range(HOPS)], axis=0)
        a = jnp.dot(lhs, rhs, preferred_element_type=f32)
        rhs = jnp.concatenate([x1l[ucols[row, h]] for h in range(HOPS)], axis=0)
        b = jnp.dot(lhs[0:BLK], rhs, preferred_element_type=f32)
        out = a[0:BLK] + a[BLK : 2 * BLK] + b
        if j < 7:
            uo[j] = out
            sends_u.append(go(remote(uo.at[j], ul.at[s], u_s.at[j], u_r.at[j], (xhi * 8 + to[j], c))))
        else:
            ul[s] = out

    jobs = {
        1: [lambda: y_job(0)],
        2: [lambda: y_job(1)],
        3: [lambda: y_job(2)] + [lambda i=i: own_convert(i) for i in range(3)],
        4: [lambda: lo_products(0, 1)] + [lambda i=i: own_convert(i) for i in range(3, 7)],
        5: [lambda: lo_products(2, 3), lambda: hi_convert(0), lambda: hi_convert(1)],
        7: [lambda: hi_convert(2), lambda: hi_convert(3)],
        9: [lambda: hi_convert(4)],
    }
    sum_vv = None
    for i, (k, h, n) in enumerate(chunks):
        rs = pl.ds(h, n)
        xl[i].wait_recv()
        if i + AHEAD < len(chunks):
            xl.append(send_x(i + AHEAD))
        xh.append(go(remote(vl.at[to[k], rs], vh.at[to[k], rs], xh_s.at[i], xh_r.at[i], dev_x3)))
        if h + n == BLK:
            row = []
            for m, dy in enumerate((1, 3, 2)):
                cp = yx_to(dy, 0)
                src = vl.at[to[k], rows_of(cp)]
                row.append(go(remote(src, x2p.at[y, to[k]], y2_s.at[k, m], y2_r.at[k, m], (r, cp))))
            y2.append(row)
        if i >= 1:
            relay_hi(i - 1)
        if i == 0:
            locals_[5].start()
            sum_vv = make_base()
            own_products(y, v.at[rows_of(c)])
            convert(r, v[:, cols_of(s)])
        for job in jobs.get(i, []):
            job()
    lo_products(4, 5)
    lo_products(6, 7)
    for j in range(EARLY):
        down_share(j)
    relay_hi(len(chunks) - 1)
    for k in range(5, 8):
        hi_convert(k)
    for j in range(8):
        up_block(j)
        if j + EARLY < 8:
            down_share(j + EARLY)

    for cp in sends_d:
        cp.wait_recv()
    locals_[5].wait()
    beta = beta_ref[0]
    zero = jnp.zeros((16, BLK), f32)
    vi, vw = zero, zero
    for k in (7, 0, 1, 2, 3, 4, 5, 6):
        if k < 7:
            sends_u[k].wait_recv()
        place = frm[k]

        def image(i, accs, place=place):
            vi, vw = accs
            rs = rows_of(i)
            for n in range(2):
                cs = pl.ds(pl.multiple_of(place * 256 + n * BLK, BLK), BLK)
                im = ul[place, rs, n * BLK : (n + 1) * BLK] + dl[i, place * 2 + n] + wbuf[rs, cs]
                w = im - beta * prev[rs, cs]
                wbuf[rs, cs] = w
                vv = v[rs, cs]
                vi = vi + vv * im
                vw = vw + vv * w
            return vi, vw

        vi, vw = lax.fori_loop(0, 8, image, (vi, vw))
    out_cp = pltpu.make_async_copy(wbuf, out_hbm, osem)
    out_cp.start()
    sum_vi, sum_vw = total_of(vi), total_of(vw)
    a_loc = ratio(sum_vw, sum_vv)

    def rest(i, accs):
        rr, rv = accs
        rs = pl.ds(pl.multiple_of(i * 16, 16), 16)
        for j in range(16):
            cs = slice(j * BLK, (j + 1) * BLK)
            vv = v[rs, cs]
            res = wbuf[rs, cs] - a_loc * vv
            rr = rr + res * res
            rv = rv + res * vv
        return rr, rv

    rr, rv = lax.fori_loop(0, 8, rest, (zero, zero))
    stats = [sum_vi, sum_vv, total_of(rr), total_of(rv), a_loc]
    lane = lax.broadcasted_iota(jnp.int32, (1, BLK), 1)

    def row_of(vals):
        row = jnp.zeros((1, BLK), f32)
        for i, x in enumerate(vals):
            row = jnp.where(lane == i, x, row)
        return row

    def merge(t):
        vis, vvs, rrs, rvs, a_s = [t[:, i : i + 1] for i in range(5)]

        def add(x):
            return jnp.sum(x, axis=0, keepdims=True)

        vv = add(vvs)
        a = ratio(add(a_s * vvs + rvs), vv)
        d = a - a_s
        return [add(vis), vv, add(rrs - 2.0 * d * rvs + d * d * vvs), add(rvs - d * vvs), a]

    g1[core] = row_of(stats)
    cp = go(remote(g1.at[core], g1.at[core], g1_s, g1_r, (xhi * 8 + z * 2 + 1 - core, c)))
    cp.wait_recv()
    stats = merge(jnp.concatenate([g1[0], g1[1]], axis=0))
    x = xhi * 2 + xlo
    chip = x * 16 + y * 4 + z
    g2[chip] = row_of(stats)

    def all_chips(act):
        def body(i, _):
            xx = lax.rem(x + lax.div(i, 4), 4)
            yy = lax.rem(y + lax.rem(i, 4), 4)
            base, col = lax.div(xx, 2) * 8 + core, yy * 2 + lax.rem(xx, 2)
            for n in range(4):
                dev = (base + lax.rem(z + n, 4) * 2, col)
                cp = remote(g2.at[chip], g2.at[chip], g2_s.at[i * 4 + n], g2_r.at[i * 4 + n], dev)
                if n > 0:
                    act(cp)
                else:
                    pl.when(i > 0)(lambda cp=cp: act(cp))
            return 0

        lax.fori_loop(0, 16, body, 0)

    all_chips(lambda cp: cp.start())
    all_chips(lambda cp: cp.wait_recv())
    for i in range(64):
        g2s[i : i + 1] = g2[i]
    vis, vvs, rrs, rvs, a = merge(g2s[...])
    alpha = vis / vvs
    d = alpha - a
    energy = rrs - 2.0 * d * rvs + d * d * vvs
    scale = jnp.sqrt(energy / (2048 * 16384) + 1e-06)
    coef[0] = alpha[0, 0]
    coef[1] = scale[0, 0]
    all_chips(lambda cp: cp.wait_send())
    for cp in started:
        cp.wait_send()
    out_cp.wait()


def finish(w_hbm, v_hbm, coef, out_hbm, coef_out, w, v, sem):
    parts = [pl.ds(i * 32, 32) for i in range(4)]
    ins = [
        [pltpu.make_async_copy(a.at[rs], b.at[rs], sem.at[n, i]) for n, (a, b) in enumerate(((w_hbm, w), (v_hbm, v)))]
        for i, rs in enumerate(parts)
    ]
    for pair in ins:
        for cp in pair:
            cp.start()
    alpha, scale = coef[0], coef[1]
    coef_out[0] = alpha
    coef_out[1] = scale
    outs = []
    for i, rs in enumerate(parts):
        for cp in ins[i]:
            cp.wait()
        w[rs] = (w[rs] - alpha * v[rs]) / scale
        outs.append(pltpu.make_async_copy(w.at[rs], out_hbm.at[rs], sem.at[2, i]))
        outs[i].start()
    for cp in outs:
        cp.wait()


def local(
    vector, previous, beta_prev, hubbard_u, up_patterns, down_patterns,
    up_cols, up_pats, down_cols, down_pats, up_occupied, down_occupied,
):
    hbm = pl.BlockSpec(memory_space=pl.ANY)
    smem = pl.BlockSpec(memory_space=pltpu.SMEM)
    dma = pltpu.SemaphoreType.DMA
    vm = pltpu.VMEM
    w, coef = pl.pallas_call(
        kernel,
        name="lanczos_step",
        out_shape=(
            jax.ShapeDtypeStruct((128, 2048), f32),
            jax.ShapeDtypeStruct((2,), f32),
        ),
        in_specs=[hbm] * 6 + [smem] * 6,
        out_specs=(hbm, smem),
        scratch_shapes=[
            vm((128, 2048), f32),
            vm((128, 2048), f32),
            vm((128, 2048), f32),
            vm((NPAT, BLK, BLK), f32),
            vm((NPAT, BLK, BLK), f32),
            vm((20, BLK), jnp.int32),
            vm((20, 2048), jnp.int32),
            vm((8, BLK, 256), f32),
            vm((8, BLK, 256), f32),
            vm((16, BLK, 256), f32),
            vm((16, BLK, 256), bf16),
            vm((16, BLK, 256), bf16),
            vm((4, 16, 2048), f32),
            vm((4, 8, 16, 256), f32),
            vm((NPAT, 3 * BLK, BLK), bf16),
            vm((NPAT, 2 * BLK, BLK), bf16),
            vm((NPAT * 128, 16, BLK), f32),
            vm((7, BLK, 256), f32),
            vm((7, 16, 16, BLK), f32),
            vm((8, BLK, 256), f32),
            vm((8, 16, 16, BLK), f32),
            vm((2, 1, BLK), f32),
            vm((64, 1, BLK), f32),
            vm((64, BLK), f32),
            dma((6,)), dma,
            dma((10,)), dma((10,)), dma((10,)), dma((10,)),
            dma((7,)), dma((7,)), dma((3,)), dma((3,)),
            dma((7,)), dma((7,)), dma((8, 3)), dma((8, 3)),
            dma((7,)), dma((7,)), dma((7,)), dma((7,)),
            dma, dma, dma((64,)), dma((64,)),
        ],
        compiler_params=pltpu.CompilerParams(
            collective_id=CID, has_side_effects=True, vmem_limit_bytes=60 << 20
        ),
    )(
        vector, previous, up_patterns, down_patterns, up_occupied, down_occupied,
        beta_prev, hubbard_u, up_cols, up_pats, down_cols.T, down_pats.T,
    )
    return pl.pallas_call(
        finish,
        name="scale_residual",
        out_shape=(
            jax.ShapeDtypeStruct((128, 2048), f32),
            jax.ShapeDtypeStruct((2,), f32),
        ),
        in_specs=[hbm, hbm, smem],
        out_specs=(hbm, smem),
        scratch_shapes=[vm((128, 2048), f32), vm((128, 2048), f32), dma((3, 4))],
        compiler_params=pltpu.CompilerParams(vmem_limit_bytes=60 << 20),
    )(w, vector, coef)


def solution(mesh):
    in_specs = (
        P("row", "col"),
        P("row", "col"),
        P(),
        P(),
        P(),
        P(),
        P(),
        P(),
        P(),
        P(),
        P(None, "row"),
        P(None, "col"),
    )
    out_specs = (P("row", "col"), P())
    return jax.shard_map(local, mesh=mesh, in_specs=in_specs, out_specs=out_specs, check_vma=False)
```

```python
import jax
import jax.numpy as jnp
from jax import lax
from jax.experimental import pallas as pl
from jax.experimental.pallas import tpu as pltpu
from jax.sharding import PartitionSpec as P

MESH = pl.DeviceIdType.MESH
f32, bf16 = jnp.float32, jnp.bfloat16
BLK = 128
CID = 0
HOPS = 12
NPAT = 16
AHEAD = 10
EARLY = 3
ZC = [(1, 0), (3, 1), (2, 0), (1, 1), (3, 0), (2, 1), (0, 1), (0, 0)]
YX = [(1, 1), (3, 1), (2, 1), (1, 0), (0, 1), (3, 0), (2, 0), (0, 0)]


def split(x):
    hi = x.astype(bf16)
    lo = (x - hi.astype(f32)).astype(bf16)
    return hi, lo


def total_of(x):
    return jnp.sum(x, axis=(0, 1), keepdims=True)


def ratio(p, q):
    return jnp.where(q > 0.0, p / jnp.where(q > 0.0, q, 1.0), 0.0)


def kernel(
    v_hbm, prev_hbm, upat_hbm, dpat_hbm, upo_hbm, dno_hbm,
    beta_ref, hub_ref, ucols, upats, dcols, dpats,
    out_hbm, coef,
    v, prev, wbuf, upat, dpat, upo, dno,
    vl, vh, x1f, x1h, x1l, x2o, x2p, dw, phl, yd,
    uo, do, ul, dl, g1, g2, g2s,
    lsem, osem, xl_s, xl_r, xh_s, xh_r, z1_s, z1_r, y1_s, y1_r, z2_s, z2_r, y2_s, y2_r,
    u_s, u_r, d_s, d_r, g1_s, g1_r, g2_s, g2_r,
):
    r, c = lax.axis_index("row"), lax.axis_index("col")
    xhi, s = lax.div(r, 8), lax.rem(r, 8)
    z, core = lax.div(s, 2), lax.rem(s, 2)
    y, xlo = lax.div(c, 2), lax.rem(c, 2)
    rhi = (1 - xhi) * 8 + s
    clo = y * 2 + 1 - xlo
    dev_lo, dev_x3 = (r, clo), (rhi, clo)

    def zc_to(k):
        dz, dc = ZC[k]
        return lax.rem(z + dz, 4) * 2 + lax.rem(core + dc, 2)

    def zc_from(k):
        dz, dc = ZC[k]
        return lax.rem(z + 4 - dz, 4) * 2 + lax.rem(core + 2 - dc, 2)

    def yx_to(dy, dx):
        return lax.rem(y + dy, 4) * 2 + lax.rem(xlo + dx, 2)

    def yx_from(dy, dx):
        return lax.rem(y + 4 - dy, 4) * 2 + lax.rem(xlo + 2 - dx, 2)

    def cols_of(k):
        return pl.ds(pl.multiple_of(k * 256, 256), 256)

    def rows_of(k):
        return pl.ds(pl.multiple_of(k * 16, 16), 16)

    def remote(src, dst, ssem, rsem, dev):
        return pltpu.make_async_remote_copy(
            src_ref=src, dst_ref=dst, send_sem=ssem, recv_sem=rsem, device_id=dev, device_id_type=MESH
        )

    locals_ = [
        pltpu.make_async_copy(a, b, lsem.at[i])
        for i, (a, b) in enumerate(
            [
                (v_hbm, v),
                (upat_hbm, upat),
                (dpat_hbm, dpat),
                (upo_hbm, upo),
                (dno_hbm, dno),
                (prev_hbm, prev),
            ]
        )
    ]
    barrier = pltpu.get_barrier_semaphore()
    peers = [(xhi * 8 + zc_to(k), c) for k in range(7)]
    peers += [(r, yx_to(dy, dx)) for dy, dx in YX[:7]]
    peers += [dev_x3]
    for dev in peers:
        pl.semaphore_signal(barrier, inc=1, device_id=dev, device_id_type=MESH)
    for cp in locals_[:5]:
        cp.start()
    pl.semaphore_wait(barrier, len(peers))

    started = []


    def go(cp):
        cp.start()
        started.append(cp)
        return cp

    to = [zc_to(k) for k in range(8)]
    frm = [zc_from(k) for k in range(8)]

    chunks = [(k, 0, BLK) for k in range(6)] + [(k, h, 64) for k in (6, 7) for h in (0, 64)]

    def send_x(i):
        k, h, n = chunks[i]
        rs = pl.ds(h, n)
        return go(remote(v_hbm.at[rs, cols_of(to[k])], vl.at[to[k], rs], xl_s.at[i], xl_r.at[i], dev_lo))

    xl = [send_x(i) for i in range(AHEAD)]
    z1, y1 = [], []
    for k in range(7):
        z1.append(
            go(remote(v_hbm.at[:, cols_of(to[k])], x1f.at[r], z1_s.at[k], z1_r.at[k], (xhi * 8 + to[k], c)))
        )
        if k < 3:
            dy = (1, 3, 2)[k]
            cp = yx_to(dy, 0)
            y1.append(go(remote(v_hbm.at[rows_of(cp)], x2o.at[y], y1_s.at[k], y1_r.at[k], (r, cp))))

    locals_[1].wait()
    locals_[2].wait()

    def prep(t, _):
        hi, lo = split(upat[t])
        phl[t, 0:BLK] = hi
        phl[t, BLK : 2 * BLK] = lo
        hi, lo = split(dpat[t].T)
        dw[t, 0:BLK] = hi
        dw[t, BLK : 2 * BLK] = hi
        dw[t, 2 * BLK : 3 * BLK] = lo
        return 0

    lax.fori_loop(0, NPAT, prep, 0)
    locals_[0].wait()

    def make_base():
        locals_[3].wait()
        locals_[4].wait()
        ups = upo[...].astype(f32).T
        hub = hub_ref[0]

        def step(i, acc):
            cs = pl.ds(pl.multiple_of(i * 256, 256), 256)
            both = jnp.dot(ups, dno[:, cs].astype(f32), preferred_element_type=f32)
            vv = v[:, cs]
            wbuf[:, cs] = hub * both * vv
            sq = vv * vv
            return acc + sum(sq[8 * a : 8 * a + 8] for a in range(16))

        acc = lax.fori_loop(0, 8, step, jnp.zeros((8, 256), f32))
        return total_of(acc)

    def products(xs, k0s, n):
        hi, lo = split(xs)
        lhs = jnp.concatenate([hi, lo, hi], axis=1)

        def step(i, _):
            rhs = jnp.concatenate([dw[i * 4 + a] for a in range(4)], axis=1)
            out = jnp.dot(lhs, rhs, preferred_element_type=f32)
            for a in range(4):
                for b, k0 in enumerate(k0s):
                    part = out[b * n * 16 : (b + 1) * n * 16, a * BLK : (a + 1) * BLK]
                    yd[pl.ds((i * 4 + a) * 128 + k0, n)] = part.reshape(n, 16, BLK)
            return 0

        lax.fori_loop(0, NPAT // 4, step, 0)

    def own_products(ysrc, ref):
        xs = jnp.concatenate([ref[:, j * BLK : (j + 1) * BLK] for j in range(16)], axis=0)
        products(xs, [(ysrc * 2 + xlo) * 16], 16)

    def lo_products(*ks):
        xs, k0s = [], []
        for k in ks:
            for i in range(3):
                y2[k][i].wait_recv()
            for dy in range(4):
                ysrc = lax.rem(y + 4 - dy, 4)
                if dy == 0:
                    piece = vl[to[k], rows_of(c)]
                else:
                    piece = x2p[ysrc, to[k]]
                xs += [piece[:, 0:BLK], piece[:, BLK : 2 * BLK]]
                k0s.append((ysrc * 2 + 1 - xlo) * 16 + to[k] * 2)
        products(jnp.concatenate(xs, axis=0), k0s, 2)

    def convert(b, x):
        hi, lo = split(x)
        x1h[b] = hi
        x1l[b] = lo

    xh, z2, y2 = [], [], []

    def relay_hi(i):
        k, h, n = chunks[i]
        xh[i].wait_recv()
        if h + n == BLK and k < 7:
            z2.append(go(remote(vh.at[to[k]], x1f.at[rhi], z2_s.at[k], z2_r.at[k], (xhi * 8 + to[k], c))))

    def hi_convert(k):
        if k < 7:
            z2[k].wait_recv()
            b = (1 - xhi) * 8 + frm[k]
            convert(b, x1f[b])
        else:
            convert(rhi, vh[s])

    def own_convert(i):
        z1[i].wait_recv()
        b = xhi * 8 + frm[i]
        convert(b, x1f[b])

    def y_job(i):
        y1[i].wait_recv()
        ysrc = lax.rem(y + 4 - (1, 3, 2)[i], 4)
        own_products(ysrc, x2o.at[ysrc])

    sends_d, sends_u = [], []

    def down_share(j):
        cp = yx_to(*YX[j])

        def block(q, _):
            for n in range(4):
                row = cp * 16 + q * 4 + n
                parts = []
                for i in range(HOPS):
                    parts.append(yd[dpats[i, row] * 128 + dcols[i, row]])
                while len(parts) > 1:
                    parts = [sum(parts[i : i + 2]) for i in range(0, len(parts), 2)]
                if j < 7:
                    do[j, q * 4 + n] = parts[0]
                else:
                    dl[c, q * 4 + n] = parts[0]
            return 0

        lax.fori_loop(0, 4, block, 0)
        if j < 7:
            sends_d.append(go(remote(do.at[j], dl.at[c], d_s.at[j], d_r.at[j], (r, cp))))

    def up_block(j):
        row = xhi * 8 + to[j]
        lhs = jnp.concatenate([phl[upats[row, h]] for h in range(HOPS)], axis=1)
        rhs = jnp.concatenate([x1h[ucols[row, h]] for h in range(HOPS)], axis=0)
        a = jnp.dot(lhs, rhs, preferred_element_type=f32)
        rhs = jnp.concatenate([x1l[ucols[row, h]] for h in range(HOPS)], axis=0)
        b = jnp.dot(lhs[0:BLK], rhs, preferred_element_type=f32)
        out = a[0:BLK] + a[BLK : 2 * BLK] + b
        if j < 7:
            uo[j] = out
            sends_u.append(go(remote(uo.at[j], ul.at[s], u_s.at[j], u_r.at[j], (xhi * 8 + to[j], c))))
        else:
            ul[s] = out

    jobs = {
        1: [lambda: y_job(0)],
        2: [lambda: y_job(1)],
        3: [lambda: y_job(2)] + [lambda i=i: own_convert(i) for i in range(3)],
        4: [lambda: lo_products(0, 1)] + [lambda i=i: own_convert(i) for i in range(3, 7)],
        5: [lambda: lo_products(2, 3), lambda: hi_convert(0), lambda: hi_convert(1)],
        7: [lambda: hi_convert(2), lambda: hi_convert(3)],
        9: [lambda: hi_convert(4)],
    }
    sum_vv = None
    for i, (k, h, n) in enumerate(chunks):
        rs = pl.ds(h, n)
        xl[i].wait_recv()
        if i + AHEAD < len(chunks):
            xl.append(send_x(i + AHEAD))
        xh.append(go(remote(vl.at[to[k], rs], vh.at[to[k], rs], xh_s.at[i], xh_r.at[i], dev_x3)))
        if h + n == BLK:
            row = []
            for m, dy in enumerate((1, 3, 2)):
                cp = yx_to(dy, 0)
                src = vl.at[to[k], rows_of(cp)]
                row.append(go(remote(src, x2p.at[y, to[k]], y2_s.at[k, m], y2_r.at[k, m], (r, cp))))
            y2.append(row)
        if i >= 1:
            relay_hi(i - 1)
        if i == 0:
            locals_[5].start()
            sum_vv = make_base()
            own_products(y, v.at[rows_of(c)])
            convert(r, v[:, cols_of(s)])
        for job in jobs.get(i, []):
            job()
    lo_products(4, 5)
    lo_products(6, 7)
    for j in range(EARLY):
        down_share(j)
    relay_hi(len(chunks) - 1)
    for k in range(5, 8):
        hi_convert(k)
    for j in range(8):
        up_block(j)
        if j + EARLY < 8:
            down_share(j + EARLY)

    for cp in sends_d:
        cp.wait_recv()
    locals_[5].wait()
    beta = beta_ref[0]
    zero = jnp.zeros((16, BLK), f32)
    vi, vw = zero, zero
    for k in (7, 0, 1, 2, 3, 4, 5, 6):
        if k < 7:
            sends_u[k].wait_recv()
        place = frm[k]

        def image(i, accs, place=place):
            vi, vw = accs
            rs = rows_of(i)
            for n in range(2):
                cs = pl.ds(pl.multiple_of(place * 256 + n * BLK, BLK), BLK)
                im = ul[place, rs, n * BLK : (n + 1) * BLK] + dl[i, place * 2 + n] + wbuf[rs, cs]
                w = im - beta * prev[rs, cs]
                wbuf[rs, cs] = w
                vv = v[rs, cs]
                vi = vi + vv * im
                vw = vw + vv * w
            return vi, vw

        vi, vw = lax.fori_loop(0, 8, image, (vi, vw))
    out_cp = pltpu.make_async_copy(wbuf, out_hbm, osem)
    out_cp.start()
    sum_vi, sum_vw = total_of(vi), total_of(vw)
    a_loc = ratio(sum_vw, sum_vv)

    def rest(i, accs):
        rr, rv = accs
        rs = pl.ds(pl.multiple_of(i * 16, 16), 16)
        for j in range(16):
            cs = slice(j * BLK, (j + 1) * BLK)
            vv = v[rs, cs]
            res = wbuf[rs, cs] - a_loc * vv
            rr = rr + res * res
            rv = rv + res * vv
        return rr, rv

    rr, rv = lax.fori_loop(0, 8, rest, (zero, zero))
    stats = [sum_vi, sum_vv, total_of(rr), total_of(rv), a_loc]
    lane = lax.broadcasted_iota(jnp.int32, (1, BLK), 1)

    def row_of(vals):
        row = jnp.zeros((1, BLK), f32)
        for i, x in enumerate(vals):
            row = jnp.where(lane == i, x, row)
        return row

    def merge(t):
        vis, vvs, rrs, rvs, a_s = [t[:, i : i + 1] for i in range(5)]

        def add(x):
            return jnp.sum(x, axis=0, keepdims=True)

        vv = add(vvs)
        a = ratio(add(a_s * vvs + rvs), vv)
        d = a - a_s
        return [add(vis), vv, add(rrs - 2.0 * d * rvs + d * d * vvs), add(rvs - d * vvs), a]

    g1[core] = row_of(stats)
    cp = go(remote(g1.at[core], g1.at[core], g1_s, g1_r, (xhi * 8 + z * 2 + 1 - core, c)))
    cp.wait_recv()
    stats = merge(jnp.concatenate([g1[0], g1[1]], axis=0))
    x = xhi * 2 + xlo
    chip = x * 16 + y * 4 + z
    g2[chip] = row_of(stats)

    def all_chips(act):
        def body(i, _):
            xx = lax.rem(x + lax.div(i, 4), 4)
            yy = lax.rem(y + lax.rem(i, 4), 4)
            base, col = lax.div(xx, 2) * 8 + core, yy * 2 + lax.rem(xx, 2)
            for n in range(4):
                dev = (base + lax.rem(z + n, 4) * 2, col)
                cp = remote(g2.at[chip], g2.at[chip], g2_s.at[i * 4 + n], g2_r.at[i * 4 + n], dev)
                if n > 0:
                    act(cp)
                else:
                    pl.when(i > 0)(lambda cp=cp: act(cp))
            return 0

        lax.fori_loop(0, 16, body, 0)

    all_chips(lambda cp: cp.start())
    all_chips(lambda cp: cp.wait_recv())
    for i in range(64):
        g2s[i : i + 1] = g2[i]
    vis, vvs, rrs, rvs, a = merge(g2s[...])
    alpha = vis / vvs
    d = alpha - a
    energy = rrs - 2.0 * d * rvs + d * d * vvs
    scale = jnp.sqrt(energy / (2048 * 16384) + 1e-06)
    coef[0] = alpha[0, 0]
    coef[1] = scale[0, 0]
    all_chips(lambda cp: cp.wait_send())
    for cp in started:
        cp.wait_send()
    out_cp.wait()


def finish(w_hbm, v_hbm, coef, out_hbm, coef_out, w, v, sem):
    parts = [pl.ds(i * 32, 32) for i in range(4)]
    ins = [
        [pltpu.make_async_copy(a.at[rs], b.at[rs], sem.at[n, i]) for n, (a, b) in enumerate(((w_hbm, w), (v_hbm, v)))]
        for i, rs in enumerate(parts)
    ]
    for pair in ins:
        for cp in pair:
            cp.start()
    alpha, scale = coef[0], coef[1]
    coef_out[0] = alpha
    coef_out[1] = scale
    outs = []
    for i, rs in enumerate(parts):
        for cp in ins[i]:
            cp.wait()
        w[rs] = (w[rs] - alpha * v[rs]) / scale
        outs.append(pltpu.make_async_copy(w.at[rs], out_hbm.at[rs], sem.at[2, i]))
        outs[i].start()
    for cp in outs:
        cp.wait()


def local(
    vector, previous, beta_prev, hubbard_u, up_patterns, down_patterns,
    up_cols, up_pats, down_cols, down_pats, up_occupied, down_occupied,
):
    hbm = pl.BlockSpec(memory_space=pl.ANY)
    smem = pl.BlockSpec(memory_space=pltpu.SMEM)
    dma = pltpu.SemaphoreType.DMA
    vm = pltpu.VMEM
    w, coef = pl.pallas_call(
        kernel,
        name="lanczos_step",
        out_shape=(
            jax.ShapeDtypeStruct((128, 2048), f32),
            jax.ShapeDtypeStruct((2,), f32),
        ),
        in_specs=[hbm] * 6 + [smem] * 6,
        out_specs=(hbm, smem),
        scratch_shapes=[
            vm((128, 2048), f32),
            vm((128, 2048), f32),
            vm((128, 2048), f32),
            vm((NPAT, BLK, BLK), f32),
            vm((NPAT, BLK, BLK), f32),
            vm((20, BLK), jnp.int32),
            vm((20, 2048), jnp.int32),
            vm((8, BLK, 256), f32),
            vm((8, BLK, 256), f32),
            vm((16, BLK, 256), f32),
            vm((16, BLK, 256), bf16),
            vm((16, BLK, 256), bf16),
            vm((4, 16, 2048), f32),
            vm((4, 8, 16, 256), f32),
            vm((NPAT, 3 * BLK, BLK), bf16),
            vm((NPAT, 2 * BLK, BLK), bf16),
            vm((NPAT * 128, 16, BLK), f32),
            vm((7, BLK, 256), f32),
            vm((7, 16, 16, BLK), f32),
            vm((8, BLK, 256), f32),
            vm((8, 16, 16, BLK), f32),
            vm((2, 1, BLK), f32),
            vm((64, 1, BLK), f32),
            vm((64, BLK), f32),
            dma((6,)), dma,
            dma((10,)), dma((10,)), dma((10,)), dma((10,)),
            dma((7,)), dma((7,)), dma((3,)), dma((3,)),
            dma((7,)), dma((7,)), dma((8, 3)), dma((8, 3)),
            dma((7,)), dma((7,)), dma((7,)), dma((7,)),
            dma, dma, dma((64,)), dma((64,)),
        ],
        compiler_params=pltpu.CompilerParams(
            collective_id=CID, has_side_effects=True, vmem_limit_bytes=60 << 20
        ),
    )(
        vector, previous, up_patterns, down_patterns, up_occupied, down_occupied,
        beta_prev, hubbard_u, up_cols, up_pats, down_cols.T, down_pats.T,
    )
    return pl.pallas_call(
        finish,
        name="scale_residual",
        out_shape=(
            jax.ShapeDtypeStruct((128, 2048), f32),
            jax.ShapeDtypeStruct((2,), f32),
        ),
        in_specs=[hbm, hbm, smem],
        out_specs=(hbm, smem),
        scratch_shapes=[vm((128, 2048), f32), vm((128, 2048), f32), dma((3, 4))],
        compiler_params=pltpu.CompilerParams(vmem_limit_bytes=60 << 20),
    )(w, vector, coef)


def solution(mesh):
    in_specs = (
        P("row", "col"),
        P("row", "col"),
        P(),
        P(),
        P(),
        P(),
        P(),
        P(),
        P(),
        P(),
        P(None, "row"),
        P(None, "col"),
    )
    out_specs = (P("row", "col"), P())
    return jax.shard_map(local, mesh=mesh, in_specs=in_specs, out_specs=out_specs, check_vma=False)
```
